256 devices in a mesh: row: 8 (over y, x_hi), col: 32 (over z, x_lo, core).
Axes of the slice: x: 4 (x_hi: 2, x_lo: 2; x = x_hi * 2 + x_lo), y: 4, z: 8, core: 2. Of those that a mesh axis runs over, the one named last changes fastest.
Arguments:
- scalar_field: float32 [256, 256, 2048], P('col', 'row'), may hold values from -1.2 to 1.2
- reaction: float32 [256, 256, 2048], P('col', 'row'), may hold values from 0.5 to 4
- x_faces: float32 [2048], replicated, may hold values from 0.5 to 4
- y_faces: float32 [256], replicated, may hold values from 0.5 to 4
- z_faces: float32 [256], replicated, may hold values from 0.5 to 4
- x_inverse: float32 [16, 128, 128], replicated, may hold values from 0 to 1, as said below
- y_inverse: float32 [2, 128, 128], replicated, may hold values from 0 to 1, as said below
- z_inverse: float32 [2, 128, 128], replicated, may hold values from 0 to 1, as said below
Outputs:
- advanced: float32 [256, 256, 2048], P('col', 'row')
The draws below stay inside these ranges and needn't reach their ends.
Inputs may be any that keep to these rules, and one draw needn't show every extreme that they name: x_inverse[c] is, up to float32 rounding, the inverse of the block of rows and columns c * 128 to (c + 1) * 128 - 1 of the matrix I - 500 A_x along one x line. y_inverse[c] is, up to float32 rounding, the inverse of the block of rows and columns c * 128 to (c + 1) * 128 - 1 of the matrix I - 500 A_y along one y line. z_inverse[c] is, up to float32 rounding, the inverse of the block of rows and columns c * 128 to (c + 1) * 128 - 1 of the matrix I - 500 A_z along one z line.
All inputs are finite; a program needn't handle non-finite values.
Results may differ from the reference program's by a relative error of at most 0.0003.
Values sent between devices are 32-bit elements; how exact they have to be, the bound alone decides.
No kernel may reach another device: no remote copies, remote signals or barrier semaphores. Data moves between devices by JAX's collectives and lax.ppermute only.
A program may use at most 64 MiB of HBM per device.

```python
import math
import jax
import jax.numpy as jnp
from jax import lax

NY = 256
NZ = 256
GROUP = 128
NX = 2048


implicit_weight = 0.5


time_step = 1000.0


def invert_small_drawn(matrix):
    order = matrix.shape[0]
    joined = jnp.concatenate([matrix, jnp.eye(order, dtype=matrix.dtype)], axis=1)

    def sweep(step_index, current):
        pivot_row = lax.dynamic_index_in_dim(current, step_index, 0, keepdims=False)
        pivot_row = pivot_row / lax.dynamic_index_in_dim(pivot_row, step_index, 0, keepdims=False)
        pivot_column = lax.dynamic_slice_in_dim(current, step_index, 1, 1)
        current = current - pivot_column * pivot_row[None, :]
        return lax.dynamic_update_index_in_dim(current, pivot_row, step_index, 0)
    joined = lax.fori_loop(0, order, sweep, joined)
    return joined[:, order:]


def faces_and_blocks(key, length):
    face_values = jnp.exp(jax.random.uniform(key, (length,), jnp.float32, math.log(0.5), math.log(4.0)))
    couple = implicit_weight * time_step * face_values
    couple_above = jnp.concatenate([couple[1:], jnp.zeros((1,), jnp.float32)])
    groups = length // GROUP
    diagonal = (1.0 + couple + couple_above).reshape(groups, GROUP)
    upper_band = couple_above.reshape(groups, GROUP)[:, :, None] * jnp.eye(GROUP, k=1, dtype=jnp.float32)
    blocks = diagonal[:, :, None] * jnp.eye(GROUP, dtype=jnp.float32) - upper_band - jnp.swapaxes(upper_band, 1, 2)
    return (face_values, jax.vmap(invert_small_drawn)(blocks))


def draw_x_faces(key, part):
    return faces_and_blocks(jax.random.fold_in(key, 101), NX)[0]


def draw_x_inverse(key, part):
    return faces_and_blocks(jax.random.fold_in(key, 101), NX)[1]


def draw_y_faces(key, part):
    return faces_and_blocks(jax.random.fold_in(key, 202), NY)[0]


def draw_y_inverse(key, part):
    return faces_and_blocks(jax.random.fold_in(key, 202), NY)[1]


def draw_z_faces(key, part):
    return faces_and_blocks(jax.random.fold_in(key, 303), NZ)[0]


def draw_z_inverse(key, part):
    return faces_and_blocks(jax.random.fold_in(key, 303), NZ)[1]


def levels(stream_key, dims, cuts, least, high):
    def one(position, parts):
        heights = jax.random.uniform(jax.random.fold_in(jax.random.fold_in(stream_key, 6), position), (parts,), jnp.float32, least / len(cuts), high / len(cuts))
        return jnp.repeat(jnp.exp(heights), dims[position] // parts).reshape((-1,) + (1,) * (len(dims) - position - 1))

    level = one(*cuts[0])
    for cut in cuts[1:]:
        level = level * one(*cut)
    return level


def setup_inputs(seed: int = 0) -> dict:
    seeds = jax.random.split(jax.random.key(seed), 9)
    return {
        "scalar_field": jnp.clip(jax.random.uniform(seeds[0], (NZ, NY, NX), jnp.float32, -1.2, 1.2) * levels(seeds[0], (NZ, NY, NX), ((0, 32), (1, 8)), -0.4, 0.0), -1.2, 1.2),
        "reaction": jnp.clip(jnp.exp(math.log(4.0) - 2.0794415 * jax.random.uniform(seeds[1], (NZ, NY, NX), jnp.float32) ** levels(seeds[1], (NZ, NY, NX), ((0, 32), (1, 8)), -0.2, 0.2)), 0.5, 4.0),
        "x_faces": draw_x_faces(jax.random.fold_in(seeds[8], 71), 0),
        "y_faces": draw_y_faces(jax.random.fold_in(seeds[8], 71), 0),
        "z_faces": draw_z_faces(jax.random.fold_in(seeds[8], 71), 0),
        "x_inverse": draw_x_inverse(jax.random.fold_in(seeds[8], 71), 0),
        "y_inverse": draw_y_inverse(jax.random.fold_in(seeds[8], 71), 0),
        "z_inverse": draw_z_inverse(jax.random.fold_in(seeds[8], 71), 0),
    }


implicit_weight = 0.5
time_step = 1000.0


def shift_lower(values, line_axis):
    length = values.shape[line_axis]
    first_slot = jnp.zeros_like(lax.slice_in_dim(values, 0, 1, axis=line_axis))
    return jnp.concatenate([first_slot, lax.slice_in_dim(values, 0, length - 1, axis=line_axis)], axis=line_axis)


def shift_upper(values, line_axis):
    length = values.shape[line_axis]
    last_slot = jnp.zeros_like(lax.slice_in_dim(values, 0, 1, axis=line_axis))
    return jnp.concatenate([lax.slice_in_dim(values, 1, length, axis=line_axis), last_slot], axis=line_axis)


def apply_line(values, face_values, line_axis):
    spread = [1, 1, 1]
    spread[line_axis] = values.shape[line_axis]
    face_here = face_values.reshape(spread)
    face_next = jnp.concatenate([face_values[1:], jnp.zeros((1,), face_values.dtype)]).reshape(spread)
    lower_value = shift_lower(values, line_axis)
    upper_value = shift_upper(values, line_axis)
    return face_next * (upper_value - values) - face_here * (values - lower_value)


def invert_small(matrix):
    order = matrix.shape[0]
    joined = jnp.concatenate([matrix, jnp.eye(order, dtype=matrix.dtype)], axis=1)

    def sweep(step_index, current):
        pivot_row = lax.dynamic_index_in_dim(current, step_index, 0, keepdims=False)
        pivot_row = pivot_row / lax.dynamic_index_in_dim(pivot_row, step_index, 0, keepdims=False)
        pivot_column = lax.dynamic_slice_in_dim(current, step_index, 1, 1)
        current = current - pivot_column * pivot_row[None, :]
        return lax.dynamic_update_index_in_dim(current, pivot_row, step_index, 0)

    joined = lax.fori_loop(0, order, sweep, joined)
    return joined[:, order:]


def reduced_inverse(inverse, coupling_before, coupling_after):
    groups, block_width = inverse.shape[0], inverse.shape[1]
    order = 2 * groups
    group_index = jnp.arange(groups)
    lead_rows = 2 * group_index
    trail_rows = 2 * group_index + 1
    prev_cols = jnp.maximum(2 * group_index - 1, 0)
    next_cols = jnp.minimum(2 * group_index + 2, order - 1)
    coupled = jnp.zeros((order, order), inverse.dtype)
    coupled = coupled.at[lead_rows, prev_cols].add(coupling_before * inverse[:, 0, 0])
    coupled = coupled.at[lead_rows, next_cols].add(coupling_after * inverse[:, 0, block_width - 1])
    coupled = coupled.at[trail_rows, prev_cols].add(coupling_before * inverse[:, block_width - 1, 0])
    coupled = coupled.at[trail_rows, next_cols].add(coupling_after * inverse[:, block_width - 1, block_width - 1])
    return invert_small(jnp.eye(order, dtype=inverse.dtype) - coupled)


def line_solve(right_side, inverse, face_values, line_axis):
    groups, block_width = inverse.shape[0], inverse.shape[1]
    dims_full = right_side.shape
    blocked = right_side.reshape(dims_full[:line_axis] + (groups, block_width) + dims_full[line_axis + 1:])
    others = ["u", "v"]
    source = "".join(others[:line_axis] + ["c", "j"] + others[line_axis:])
    target = "".join(others[:line_axis] + ["c", "i"] + others[line_axis:])
    inside = jnp.einsum("cij," + source + "->" + target, inverse, blocked, precision=lax.Precision.HIGHEST)
    leading = lax.index_in_dim(inside, 0, line_axis + 1, keepdims=False)
    trailing = lax.index_in_dim(inside, block_width - 1, line_axis + 1, keepdims=False)
    coupling = implicit_weight * time_step * face_values[block_width::block_width]
    nothing = jnp.zeros((1,), face_values.dtype)
    coupling_before = jnp.concatenate([nothing, coupling])
    coupling_after = jnp.concatenate([coupling, nothing])
    reduced = reduced_inverse(inverse, coupling_before, coupling_after)
    interface = jnp.stack([leading, trailing], axis=line_axis + 1)
    interface = interface.reshape(dims_full[:line_axis] + (2 * groups,) + dims_full[line_axis + 1:])
    end_source = "".join(others[:line_axis] + ["j"] + others[line_axis:])
    end_target = "".join(others[:line_axis] + ["i"] + others[line_axis:])
    solved = jnp.einsum("ij," + end_source + "->" + end_target, reduced, interface, precision=lax.Precision.HIGHEST)
    solved = solved.reshape(dims_full[:line_axis] + (groups, 2) + dims_full[line_axis + 1:])
    first_values = lax.index_in_dim(solved, 0, line_axis + 1, keepdims=False)
    last_values = lax.index_in_dim(solved, 1, line_axis + 1, keepdims=False)
    prev_last = shift_lower(last_values, line_axis)
    next_first = shift_upper(first_values, line_axis)
    spike_shape = [1, 1, 1, 1]
    spike_shape[line_axis] = groups
    spike_shape[line_axis + 1] = block_width
    left_spike = (coupling_before[:, None] * inverse[:, :, 0]).reshape(spike_shape)
    right_spike = (coupling_after[:, None] * inverse[:, :, block_width - 1]).reshape(spike_shape)
    result = inside + left_spike * jnp.expand_dims(prev_last, line_axis + 1) + right_spike * jnp.expand_dims(next_first, line_axis + 1)
    return result.reshape(dims_full)


def reference(scalar_field, reaction, x_faces, y_faces, z_faces, x_inverse, y_inverse, z_inverse):
    x_term = apply_line(scalar_field, x_faces, 2)
    y_term = apply_line(scalar_field, y_faces, 1)
    z_term = apply_line(scalar_field, z_faces, 0)
    source = reaction * scalar_field * (1.0 - scalar_field * scalar_field)
    explicit = scalar_field + time_step * (x_term + y_term + z_term + source) - implicit_weight * time_step * x_term
    first_section = line_solve(explicit, x_inverse, x_faces, 2)
    second_section = line_solve(first_section - implicit_weight * time_step * y_term, y_inverse, y_faces, 1)
    return line_solve(second_section - implicit_weight * time_step * z_term, z_inverse, z_faces, 0)
```

```python
import functools

import jax
import jax.numpy as jnp
from jax import lax
from jax.experimental import pallas as pl
from jax.experimental.pallas import tpu as pltpu
from jax.sharding import PartitionSpec as P

F32 = jnp.float32
half_step = 500.0
time_step = 1000.0
LANES = 128


def dot(left, right):
    return lax.dot_general(
        left,
        right,
        (((1,), (0,)), ((), ())),
        precision=lax.Precision.HIGHEST,
        preferred_element_type=F32,
    )


def dot_t(left, right):
    return lax.dot_general(
        left,
        right,
        (((1,), (1,)), ((), ())),
        precision=lax.Precision.HIGHEST,
        preferred_element_type=F32,
    )


def iota(shape, dim):
    return lax.broadcasted_iota(jnp.int32, shape, dim)


def joint(g_ref, faces_ref):
    b = half_step * faces_ref[0:1, 128:129]
    g0 = g_ref[0, 127:128, 127:128]
    g1 = g_ref[1, 0:1, 0:1]
    den = 1.0 - b * b * g0 * g1
    return b * b * g1 / den, b * b * g0 / den, b / den


def line_block(g_ref, faces_ref, start, size):
    alpha0, alpha1, _ = joint(g_ref, faces_ref)
    group = start // 128
    offset = start - group * 128
    rows = g_ref[group, pl.ds(pl.multiple_of(offset, size), size), :]
    low = group == 0
    edge_row = jnp.where(low, g_ref[0, 127:128, :], g_ref[1, 0:1, :])
    edge_col = jnp.where(low, rows[:, 127:128], rows[:, 0:1])
    alpha = jnp.where(low, alpha0, alpha1)
    block = rows + (alpha * edge_col) * edge_row
    return pltpu.roll(block, lax.rem(128 - offset, 128), 1)


def element(g_ref, joined, i, j):
    alpha0, alpha1, beta = joined
    gi, gj = i // 128, j // 128
    li, lj = i % 128, j % 128
    ei, ej = (0 if gi else 127), (0 if gj else 127)
    across = g_ref[gi, li : li + 1, ei : ei + 1] * g_ref[gj, ej : ej + 1, lj : lj + 1]
    if gi == gj:
        alpha = alpha1 if gi else alpha0
        return g_ref[gi, li : li + 1, lj : lj + 1] + alpha * across
    return beta * across


def call(kernel, out_shape, flops, nbytes, name, **kw):
    return pl.pallas_call(
        kernel,
        out_shape=out_shape,
        name=name,
        compiler_params=pltpu.CompilerParams(vmem_limit_bytes=48 * 1024 * 1024),
        cost_estimate=pl.CostEstimate(flops=flops, bytes_accessed=nbytes, transcendentals=0),
        **kw,
    )


def explicit_kernel(u_ref, r_ref, xf_ref, gy_ref, yf_ref, a_ref, buf_ref, w_ref):
    z = pl.program_id(0)
    cells = u_ref.shape[1]
    width = u_ref.shape[2]

    @pl.when(z == 0)
    def _():
        block = line_block(gy_ref, yf_ref, lax.axis_index("row") * cells, cells)
        last = block[:, cells - 1 : cells] / block[cells - 1 : cells, cells - 1 : cells]
        first = block[:, 0:1] / block[0:1, 0:1]
        w_ref[0] = jnp.broadcast_to(last, (cells, LANES))
        w_ref[1] = jnp.broadcast_to(first, (cells, LANES))

    u = u_ref[0]
    here = xf_ref[...]
    lane = iota((1, width), 1)
    after = jnp.where(lane == width - 1, 0.0, pltpu.roll(here, width - 1, 1))
    lower = jnp.where(iota((cells, width), 1) == 0, 0.0, pltpu.roll(u, 1, 1))
    upper = pltpu.roll(u, width - 1, 1)
    x_term = after * (upper - u) - here * (u - lower)
    a = time_step * (x_term + r_ref[0] * u * (1.0 - u * u)) + 4.0 * u
    a_ref[0] = a
    dests, span = buf_ref.shape[0], buf_ref.shape[2]
    for d in range(dests):
        for k in range(2):
            w = w_ref[k, :, 0:1]
            for f, field in enumerate((a, u)):
                part = field[:, d * span : (d + 1) * span]
                row = jnp.sum(w * part, axis=0, keepdims=True)
                buf_ref[d, pl.ds(z + 16 * k + 8 * f, 1), :] = row


def coef_kernel(gy_ref, yf_ref, gz_ref, zf_ref, yc_ref, zc_ref):
    for g_ref, f_ref, out_ref, count in ((gy_ref, yf_ref, yc_ref, 8), (gz_ref, zf_ref, zc_ref, 16)):
        joined = joint(g_ref, f_ref)
        size = 256 // count
        m = functools.partial(element, g_ref, joined)
        out_ref[...] = jnp.zeros_like(out_ref)
        for c in range(count):
            b, e = c * size, c * size + size - 1
            if c > 0:
                ee = m(e, e - size) / m(e, e)
                be = m(b, b - 1)
                out_ref[c : c + 1, :] = jnp.broadcast_to(ee, (1, LANES))
                out_ref[count + c : count + c + 1, :] = jnp.broadcast_to(be, (1, LANES))
            if c < count - 1:
                bb = m(b, b + size) / m(b, b)
                eb = m(e, e + 1)
                out_ref[2 * count + c : 2 * count + c + 1, :] = jnp.broadcast_to(bb, (1, LANES))
                out_ref[3 * count + c : 3 * count + c + 1, :] = jnp.broadcast_to(eb, (1, LANES))


def scan_kernel(in_ref, c_ref, out_ref):
    count, rows, span = in_ref.shape
    half = rows // 2

    def coef(k):
        return c_ref[k : k + 1, 0:1]

    zero = jnp.zeros((half, span), F32)
    out_ref[0, :half, :] = zero
    out_ref[count - 1, half:, :] = zero
    below = above = None
    for s in range(count - 1):
        own = in_ref[s, :half, :]
        below = own if s == 0 else own + coef(s) * below
        out_ref[s + 1, :half, :] = coef(count + s + 1) * below
        t = count - 1 - s
        own = in_ref[t, half:, :]
        above = own if s == 0 else own + coef(2 * count + t) * above
        out_ref[t - 1, half:, :] = coef(3 * count + t - 1) * above


def local_kernel(a_ref, u_ref, gy_ref, yf_ref, gz_ref, zf_ref, l_ref, zp_ref, k_ref):
    planes, cells = a_ref.shape[0], a_ref.shape[1]
    local = planes * cells

    @pl.when(pl.program_id(0) == 0)
    def _():
        dy = line_block(gy_ref, yf_ref, lax.axis_index("row") * cells, cells)
        dz = line_block(gz_ref, zf_ref, lax.axis_index("col") * planes, planes)
        spread_y = (iota((LANES, local), 0) == iota((LANES, local), 1) % cells).astype(F32)
        spread_z = (iota((LANES, local), 0) == iota((LANES, local), 1) // cells).astype(F32)
        dy_tiled = dot(dy, spread_y)
        unit = (iota((cells, local), 0) == iota((cells, local), 1) % cells).astype(F32)
        last = dz[planes - 1 : planes, :] / dz[planes - 1 : planes, planes - 1 : planes]
        first = dz[0:1, :] / dz[0:1, 0:1]
        rows = jnp.concatenate([dz, last, first, jnp.zeros((6, LANES), F32)], axis=0)
        wide = dot(rows, spread_z)
        plane = iota((1, local), 1) // cells
        for k in range(planes + 2):
            row = wide[k : k + 1, :]
            k_ref[k * cells : (k + 1) * cells, :local] = dy_tiled * row
            other = unit * row
            if k < planes:
                other = other + jnp.where(plane == k, dy_tiled, 0.0)
            k_ref[k * cells : (k + 1) * cells, local:] = -2.0 * other

    span = a_ref.shape[2]
    both = jnp.concatenate(
        [a_ref[...].reshape(local, span), u_ref[...].reshape(local, span)], axis=0
    )
    out = dot(k_ref[...], both)
    l_ref[...] = out[:local, :]
    zp_ref[...] = out[local:, :]


def reduced_kernel(g_ref, xf_ref, et_ref, b_ref):
    groups, width = g_ref.shape[0], g_ref.shape[1]
    order = 2 * groups
    shape = (order, LANES)
    row, col = iota(shape, 0), iota(shape, 1)
    current = ((row == col) | (row + order == col)).astype(F32)
    couple = [half_step * xf_ref[0:1, width * c : width * c + 1] for c in range(1, groups)]
    et_ref[...] = jnp.zeros_like(et_ref)
    for c in range(groups):
        span = slice(c * width, (c + 1) * width)
        first_row, last_row = g_ref[c, 0:1, :], g_ref[c, width - 1 : width, :]
        et_ref[2 * c : 2 * c + 1, span] = first_row
        et_ref[2 * c + 1 : 2 * c + 2, span] = last_row
        if c > 0:
            at = row == 2 * c - 1
            b = couple[c - 1]
            current = current - jnp.where(at & (col == 2 * c), b * first_row[:, 0:1], 0.0)
            current = current - jnp.where(at & (col == 2 * c + 1), b * last_row[:, 0:1], 0.0)
        if c < groups - 1:
            at = row == 2 * c + 2
            b = couple[c]
            current = current - jnp.where(
                at & (col == 2 * c), b * first_row[:, width - 1 : width], 0.0
            )
            current = current - jnp.where(
                at & (col == 2 * c + 1), b * last_row[:, width - 1 : width], 0.0
            )
    for s in range(order):
        pivot = current[s : s + 1, :] / current[s : s + 1, s : s + 1]
        current = jnp.where(row == s, pivot, current - current[:, s : s + 1] * pivot)
    for c in range(groups):
        span = slice(c * width, (c + 1) * width)
        add = jnp.zeros((order, width), F32)
        if c > 0:
            k = order + 2 * c - 1
            add = add + current[:, k : k + 1] * (couple[c - 1] * g_ref[c, 0:1, :])
        if c < groups - 1:
            k = order + 2 * c + 2
            add = add + current[:, k : k + 1] * (couple[c] * g_ref[c, width - 1 : width, :])
        b_ref[:, span] = add


def x_solve(rows_ref, g_ref, et_ref, b_ref, store):
    groups, width = g_ref.shape[0], g_ref.shape[1]
    ends = dot_t(rows_ref[...], et_ref[...])
    for c in range(groups):
        span = slice(c * width, (c + 1) * width)
        store(span, dot_t(rows_ref[:, span], g_ref[c]) + dot(ends, b_ref[:, span]))


def section_kernel(
    y_ref, zp_ref, gy_ref, yf_ref, gz_ref, zf_ref, keep_ref, send_ref, all_ref
):
    blocks, rows, span = y_ref.shape
    cells = zp_ref.shape[0] // 2
    planes = rows // 4
    mine = lax.axis_index("col") % 2
    dy = line_block(gy_ref, yf_ref, lax.axis_index("row") * cells, cells)
    dz = line_block(gz_ref, zf_ref, lax.axis_index("col") * planes, planes)
    from_last = dy[:, cells - 1 : cells] / dy[cells - 1 : cells, cells - 1 : cells]
    from_first = dy[:, 0:1] / dy[0:1, 0:1]
    last = dz[:, planes - 1 : planes] / dz[planes - 1 : planes, planes - 1 : planes]
    first = dz[:, 0:1] / dz[0:1, 0:1]
    for s in range(blocks):
        at = slice(s * span, (s + 1) * span)
        below = y_ref[s, 0:planes, :]
        above = y_ref[s, 2 * planes : 3 * planes, :]
        for k, w in enumerate((last, first)):
            lo = jnp.sum(w * below, axis=0, keepdims=True)
            hi = jnp.sum(w * above, axis=0, keepdims=True)
            own = slice(k * cells, (k + 1) * cells)
            all_ref[own, at] = zp_ref[own, at] + from_first * lo + from_last * hi
    half = cells // 2
    for k in range(2):
        at = slice(k * half, (k + 1) * half)
        kept = pl.multiple_of(k * cells + mine * half, half)
        sent = pl.multiple_of(k * cells + (1 - mine) * half, half)
        keep_ref[at, :] = all_ref[pl.ds(kept, half), :]
        send_ref[at, :] = all_ref[pl.ds(sent, half), :]


def chip_pair(keep_ref, recv_ref, rows, lanes):
    lower_core = lax.axis_index("col") % 2 == 0
    kept, got = keep_ref[rows, lanes], recv_ref[rows, lanes]
    return jnp.where(lower_core, kept, got), jnp.where(lower_core, got, kept)


def pack_kernel(planes, keep_ref, recv_ref, gz_ref, zf_ref, buf_ref):
    chip = 2 * planes
    block = line_block(gz_ref, zf_ref, lax.axis_index("col") // 2 * chip, chip)
    e0, e1 = planes - 1, chip - 1
    up = block[e1 : e1 + 1, e0 : e0 + 1] / block[e1 : e1 + 1, e1 : e1 + 1]
    down = block[0:1, planes : planes + 1] / block[0:1, 0:1]
    dests, rows, span = buf_ref.shape
    half = rows // 2
    for d in range(dests):
        lanes = slice(d * span, (d + 1) * span)
        p0, p1 = chip_pair(keep_ref, recv_ref, slice(0, half), lanes)
        buf_ref[d, :half, :] = p1 + up * p0
        q0, q1 = chip_pair(keep_ref, recv_ref, slice(half, rows), lanes)
        buf_ref[d, half:, :] = q0 + down * q1


def unpack_kernel(planes, back_ref, keep_ref, recv_ref, gz_ref, zf_ref, own_ref, sib_ref):
    chip = 2 * planes
    block = line_block(gz_ref, zf_ref, lax.axis_index("col") // 2 * chip, chip)
    e0, b1, e1 = planes - 1, planes, chip - 1
    up = block[b1 : b1 + 1, 0:1] / block[0:1, 0:1]
    down = block[e0 : e0 + 1, e1 : e1 + 1] / block[e1 : e1 + 1, e1 : e1 + 1]
    cross = block[b1 : b1 + 1, e0 : e0 + 1]
    lower_core = lax.axis_index("col") % 2 == 0
    dests, rows, span = back_ref.shape
    half = rows // 2
    for d in range(dests):
        lanes = slice(d * span, (d + 1) * span)
        p0, _ = chip_pair(keep_ref, recv_ref, slice(0, half), lanes)
        _, q1 = chip_pair(keep_ref, recv_ref, slice(half, rows), lanes)
        below0 = back_ref[d, :half, :]
        below1 = up * below0 + cross * p0
        above1 = back_ref[d, half:, :]
        above0 = down * above1 + cross * q1
        own_ref[:half, lanes] = jnp.where(lower_core, below0, below1)
        own_ref[half:, lanes] = jnp.where(lower_core, above0, above1)
        sib_ref[:half, lanes] = jnp.where(lower_core, below1, below0)
        sib_ref[half:, lanes] = jnp.where(lower_core, above1, above0)


def inner_kernel(
    l_ref, y_ref, u_ref, gy_ref, yf_ref, gz_ref, zf_ref, gx_ref, et_ref, b_ref, out_ref, rows_ref
):
    blocks, rows, span = y_ref.shape
    planes = rows // 4
    cells = u_ref.shape[1]
    local = planes * cells
    dy = line_block(gy_ref, yf_ref, lax.axis_index("row") * cells, cells)
    dz = line_block(gz_ref, zf_ref, lax.axis_index("col") * planes, planes)
    from_last = dy[:, cells - 1 : cells] / dy[cells - 1 : cells, cells - 1 : cells]
    from_first = dy[:, 0:1] / dy[0:1, 0:1]
    lane = iota((1, LANES), 1)
    parts = []
    for z in range(planes):
        row = jnp.where(lane < planes, dz[z : z + 1, :], jnp.where(lane == planes + z, -2.0, 0.0))
        parts.append(from_first * row + from_last * pltpu.roll(row, 2 * planes, 1))
    mix = jnp.concatenate(parts, axis=0)[:, :rows]
    for s in range(blocks):
        at = slice(s * span, (s + 1) * span)
        rows_ref[:, at] = l_ref[:, at] + dot(mix, y_ref[s])

    def store(at, value):
        for z in range(planes):
            out_ref[z, :, at] = u_ref[z, :, at] + value[z * cells : (z + 1) * cells, :]

    x_solve(rows_ref, gx_ref, et_ref, b_ref, store)


def final_kernel(
    s_ref, own_ref, got_ref, gz_ref, zf_ref, gx_ref, et_ref, b_ref, out_ref, x_ref, sx_ref, c_ref
):
    z = pl.program_id(0)
    planes = c_ref.shape[1]
    cells = s_ref.shape[1]
    half = cells // 2

    @pl.when(z == 0)
    def _():
        mine = lax.axis_index("col") % 2
        for k in range(2):
            at = slice(k * half, (k + 1) * half)
            own = pl.multiple_of(k * cells + mine * half, half)
            other = pl.multiple_of(k * cells + (1 - mine) * half, half)
            x_ref[pl.ds(own, half), :] = own_ref[at, :]
            x_ref[pl.ds(other, half), :] = got_ref[at, :]
        dz = line_block(gz_ref, zf_ref, lax.axis_index("col") * planes, planes)
        first = dz[:, 0:1] / dz[0:1, 0:1]
        last = dz[:, planes - 1 : planes] / dz[planes - 1 : planes, planes - 1 : planes]
        c_ref[0] = jnp.broadcast_to(first, (planes, LANES))
        c_ref[1] = jnp.broadcast_to(last, (planes, LANES))

        def store(at, value):
            sx_ref[:, at] = value

        x_solve(x_ref, gx_ref, et_ref, b_ref, store)

    low = c_ref[0, pl.ds(z, 1), :][:, 0:1]
    high = c_ref[1, pl.ds(z, 1), :][:, 0:1]
    out_ref[0] = s_ref[0] + low * sx_ref[:cells, :] + high * sx_ref[cells:, :]


def body(scalar_field, reaction, x_faces, y_faces, z_faces, x_inverse, y_inverse, z_inverse):
    planes, cells, width = scalar_field.shape
    local = planes * cells
    rows = lax.axis_size("row")
    chips = lax.axis_size("col") // 2
    xf, yf, zf = x_faces[None, :], y_faces[None, :], z_faces[None, :]
    sds = lambda *s: jax.ShapeDtypeStruct(s, F32)
    whole = lambda *s: pl.BlockSpec(s, lambda i: (0,) * len(s))
    plane = pl.BlockSpec((1, cells, width), lambda i: (i, 0, 0))
    gspec, fspec = whole(2, 128, 128), whole(1, 256)

    a, y_buf = call(
        explicit_kernel,
        (sds(planes, cells, width), sds(rows, 4 * planes, width // rows)),
        20 * local * width,
        12 * local * width,
        "explicit",
        grid=(planes,),
        in_specs=[plane, plane, whole(1, width), gspec, fspec],
        out_specs=(plane, whole(rows, 4 * planes, width // rows)),
        scratch_shapes=[pltpu.VMEM((2, cells, LANES), F32)],
    )(scalar_field, reaction, xf, y_inverse, yf)
    y_in = lax.all_to_all(y_buf, "row", 0, 0, tiled=True)

    y_coef, z_coef = call(coef_kernel, (sds(32, LANES), sds(64, LANES)), 10**8, 10**6, "coefs")(
        y_inverse, yf, z_inverse, zf
    )
    end_rows, end_adds = call(
        reduced_kernel, (sds(32, width), sds(32, width)), 10**9, 2 * 10**6, "reduced"
    )(x_inverse, xf)
    span = 512
    chunk = pl.BlockSpec((planes, cells, span), lambda i: (0, 0, i))
    inside, z_part = call(
        local_kernel,
        (sds(local, width), sds(2 * cells, width)),
        12 * 320 * 512 * width,
        14 * local * width,
        "local",
        grid=(width // span,),
        in_specs=[chunk, chunk, gspec, fspec, gspec, fspec],
        out_specs=(
            pl.BlockSpec((local, span), lambda i: (0, i)),
            pl.BlockSpec((2 * cells, span), lambda i: (0, i)),
        ),
        scratch_shapes=[pltpu.VMEM((local + 2 * cells, 2 * local), F32)],
    )(a, scalar_field, y_inverse, yf, z_inverse, zf)

    y_out = call(scan_kernel, sds(*y_in.shape), 10**6, 10**6, "scan_y")(y_in, y_coef)
    y_back = lax.all_to_all(y_out, "row", 0, 0, tiled=True)

    keep, send = call(
        section_kernel,
        (sds(cells, width), sds(cells, width)),
        10**7,
        10**6,
        "section",
        scratch_shapes=[pltpu.VMEM((2 * cells, width), F32)],
    )(y_back, z_part, y_inverse, yf, z_inverse, zf)
    pairs = [(i, i ^ 1) for i in range(2 * chips)]
    recv = lax.ppermute(send, "col", pairs)
    z_buf = call(
        functools.partial(pack_kernel, planes), sds(chips, cells, width // chips), 10**6, 10**6, "pack"
    )(keep, recv, z_inverse, zf)
    groups = [list(range(k, 2 * chips, 2)) for k in range(2)]
    z_in = lax.all_to_all(z_buf, "col", 0, 0, axis_index_groups=groups, tiled=True)

    partial_out = call(
        inner_kernel,
        sds(planes, cells, width),
        12 * local * width * 200,
        16 * local * width,
        "inner",
        scratch_shapes=[pltpu.VMEM((local, width), F32)],
    )(
        inside, y_back, scalar_field, y_inverse, yf, z_inverse, zf, x_inverse, end_rows, end_adds
    )

    z_out = call(scan_kernel, sds(*z_in.shape), 10**6, 10**6, "scan_z")(z_in, z_coef)
    z_back = lax.all_to_all(z_out, "col", 0, 0, axis_index_groups=groups, tiled=True)
    own, sib = call(
        functools.partial(unpack_kernel, planes),
        (sds(cells, width), sds(cells, width)),
        10**6,
        10**6,
        "unpack",
    )(z_back, keep, recv, z_inverse, zf)
    got = lax.ppermute(sib, "col", pairs)
    return call(
        final_kernel,
        sds(planes, cells, width),
        12 * local * width,
        8 * local * width,
        "final",
        grid=(planes,),
        in_specs=[
            plane,
            whole(cells, width),
            whole(cells, width),
            gspec,
            fspec,
            whole(*x_inverse.shape),
            whole(32, width),
            whole(32, width),
        ],
        out_specs=plane,
        scratch_shapes=[
            pltpu.VMEM((2 * cells, width), F32),
            pltpu.VMEM((2 * cells, width), F32),
            pltpu.VMEM((2, planes, LANES), F32),
        ],
    )(partial_out, own, got, z_inverse, zf, x_inverse, end_rows, end_adds)


def solution(mesh):
    in_specs = (P("col", "row", None), P("col", "row", None), P(), P(), P(), P(), P(), P())
    out_specs = P("col", "row", None)
    return jax.shard_map(body, mesh=mesh, in_specs=in_specs, out_specs=out_specs, check_vma=False)
```

```python
import functools

import jax
import jax.numpy as jnp
from jax import lax
from jax.experimental import pallas as pl
from jax.experimental.pallas import tpu as pltpu
from jax.sharding import Mesh
from jax.sharding import PartitionSpec as P

F32 = jnp.float32
BF16 = jnp.bfloat16
half_step = 500.0
time_step = 1000.0
LANES = 128


def dot(left, right):
    return lax.dot_general(
        left,
        right,
        (((1,), (0,)), ((), ())),
        precision=lax.Precision.HIGHEST,
        preferred_element_type=F32,
    )


def halves(value):
    high = value.astype(BF16)
    return high, (value - high.astype(F32)).astype(BF16)


def iota(shape, dim):
    return lax.broadcasted_iota(jnp.int32, shape, dim)


def joint(g_ref, faces_ref):
    b = half_step * faces_ref[0:1, 128:129]
    g0 = g_ref[0, 127:128, 127:128]
    g1 = g_ref[1, 0:1, 0:1]
    den = 1.0 - b * b * g0 * g1
    return b * b * g1 / den, b * b * g0 / den, b / den


def line_block(g_ref, faces_ref, start, size):
    alpha0, alpha1, _ = joint(g_ref, faces_ref)
    group = start // 128
    offset = start - group * 128
    rows = g_ref[group, pl.ds(pl.multiple_of(offset, size), size), :]
    low = group == 0
    edge_row = jnp.where(low, g_ref[0, 127:128, :], g_ref[1, 0:1, :])
    edge_col = jnp.where(low, rows[:, 127:128], rows[:, 0:1])
    alpha = jnp.where(low, alpha0, alpha1)
    block = rows + (alpha * edge_col) * edge_row
    return pltpu.roll(block, lax.rem(128 - offset, 128), 1)


def element(g_ref, joined, i, j):
    alpha0, alpha1, beta = joined
    gi, gj = i // 128, j // 128
    li, lj = i % 128, j % 128
    ei, ej = (0 if gi else 127), (0 if gj else 127)
    across = g_ref[gi, li : li + 1, ei : ei + 1] * g_ref[gj, ej : ej + 1, lj : lj + 1]
    if gi == gj:
        alpha = alpha1 if gi else alpha0
        return g_ref[gi, li : li + 1, lj : lj + 1] + alpha * across
    return beta * across


MIB = 1024 * 1024


def call(kernel, out_shape, flops, nbytes, name, room=20, **kw):
    return pl.pallas_call(
        kernel,
        out_shape=out_shape,
        name=name,
        compiler_params=pltpu.CompilerParams(vmem_limit_bytes=int(room * MIB)),
        cost_estimate=pl.CostEstimate(flops=flops, bytes_accessed=nbytes, transcendentals=0),
        **kw,
    )


def call_after(earlier, kernel, out_shape, flops, nbytes, name, *args, **kw):
    count, extra = len(args), len(earlier)

    def ordered(*refs):
        kernel(*refs[:count], *refs[count + extra :])

    specs = [pl.BlockSpec(memory_space=pltpu.VMEM)] * count + [pl.BlockSpec(memory_space=pltpu.HBM)] * extra
    return call(ordered, out_shape, flops, nbytes, name, in_specs=specs, **kw)(*args, *earlier)


def explicit_kernel(
    u_hbm, r_hbm, xf_hbm, gy_hbm, yf_hbm, a_hbm, buf_ref,
    u_ref, r_ref, a_ref, xf_ref, gy_ref, yf_ref, f_ref, u_sem, r_sem, a_sem, s_sem
):
    planes, cells, width = u_ref.shape
    small = [
        pltpu.make_async_copy(gy_hbm, gy_ref, s_sem.at[0]),
        pltpu.make_async_copy(yf_hbm, yf_ref, s_sem.at[1]),
        pltpu.make_async_copy(xf_hbm, xf_ref, s_sem.at[2]),
    ]
    for copy in small:
        copy.start()

    def fetch(z):
        return (
            pltpu.make_async_copy(u_hbm.at[z], u_ref.at[z], u_sem.at[z]),
            pltpu.make_async_copy(r_hbm.at[z], r_ref.at[z], r_sem.at[z]),
        )

    def give(z):
        return pltpu.make_async_copy(a_ref.at[z], a_hbm.at[z], a_sem.at[z])

    for z in range(planes):
        for copy in fetch(z):
            copy.start()
    for copy in small:
        copy.wait()

    block = line_block(gy_ref, yf_ref, lax.axis_index("row") * cells, cells)
    last = block[:, cells - 1 : cells] / block[cells - 1 : cells, cells - 1 : cells]
    first = block[:, 0:1] / block[0:1, 0:1]
    w = [jnp.broadcast_to(v, (cells, LANES)) for v in (last, first)]
    here = time_step * xf_ref[...]
    lane = iota((1, width), 1)
    after = jnp.where(lane == width - 1, 0.0, pltpu.roll(here, width - 1, 1))
    f_ref[0:1, :] = after
    f_ref[1:2, :] = jnp.where(lane == 0, 0.0, here)
    f_ref[2:3, :] = 4.0 - (after + here)

    span = buf_ref.shape[2]
    count = width // LANES
    lane = iota((cells, LANES), 1)

    def plane(z, carry):
        for copy in fetch(z):
            copy.wait()

        def column(c):
            here = u_ref[z, :, c * LANES : (c + 1) * LANES]
            return here, pltpu.roll(here, 1, 1), pltpu.roll(here, LANES - 1, 1)

        sums = {}
        before = jnp.zeros((cells, LANES), F32)
        now = column(0)
        for c in range(count):
            then = column(c + 1) if c + 1 < count else (None, None, before)
            u = now[0]
            lower = jnp.where(lane == 0, before, now[1])
            upper = jnp.where(lane == LANES - 1, then[2], now[2])
            at = slice(c * LANES, (c + 1) * LANES)
            rate = r_ref[z, :, at] * (time_step - time_step * (u * u)) + f_ref[2:3, at]
            a = f_ref[0:1, at] * upper + f_ref[1:2, at] * lower + rate * u
            a_ref[z, :, at] = a
            for k in range(2):
                for f, field in enumerate((a, u)):
                    row = jnp.sum(w[k] * field, axis=0, keepdims=True)
                    sums.setdefault((k, f), []).append(row)
            if (c + 1) * LANES % span == 0:
                for (k, f), pieces in sums.items():
                    row = jnp.concatenate(pieces, axis=1)
                    buf_ref[c * LANES // span, pl.ds(z + 16 * k + 8 * f, 1), :] = row
                sums = {}
            before, now = now[1], then
        give(z).start()
        return carry

    lax.fori_loop(0, planes, plane, 0)
    for z in range(planes):
        give(z).wait()


def coef_kernel(gy_ref, yf_ref, gz_ref, zf_ref, yc_ref, zc_ref):
    for g_ref, f_ref, out_ref, count in ((gy_ref, yf_ref, yc_ref, 8), (gz_ref, zf_ref, zc_ref, 16)):
        joined = joint(g_ref, f_ref)
        size = 256 // count
        m = functools.partial(element, g_ref, joined)
        out_ref[...] = jnp.zeros_like(out_ref)
        for c in range(count):
            b, e = c * size, c * size + size - 1
            if c > 0:
                ee = m(e, e - size) / m(e, e)
                be = m(b, b - 1)
                out_ref[c : c + 1, :] = jnp.broadcast_to(ee, (1, LANES))
                out_ref[count + c : count + c + 1, :] = jnp.broadcast_to(be, (1, LANES))
            if c < count - 1:
                bb = m(b, b + size) / m(b, b)
                eb = m(e, e + 1)
                out_ref[2 * count + c : 2 * count + c + 1, :] = jnp.broadcast_to(bb, (1, LANES))
                out_ref[3 * count + c : 3 * count + c + 1, :] = jnp.broadcast_to(eb, (1, LANES))


def scan_kernel(in_ref, c_ref, out_ref):
    count, rows, span = in_ref.shape
    half = rows // 2

    def coef(k):
        return c_ref[k : k + 1, 0:1]

    zero = jnp.zeros((half, span), F32)
    out_ref[0, :half, :] = zero
    out_ref[count - 1, half:, :] = zero
    below = above = None
    for s in range(count - 1):
        own = in_ref[s, :half, :]
        below = own if s == 0 else own + coef(s) * below
        out_ref[s + 1, :half, :] = coef(count + s + 1) * below
        t = count - 1 - s
        own = in_ref[t, half:, :]
        above = own if s == 0 else own + coef(2 * count + t) * above
        out_ref[t - 1, half:, :] = coef(3 * count + t - 1) * above


def local_kernel(
    a_hbm, u_hbm, gy_ref, yf_ref, gz_ref, zf_ref, l_hbm, zp_ref,
    k_ref, a_ref, u_ref, l_ref, a_sem, u_sem, l_sem
):
    chunks, planes, cells, span = u_ref.shape

    def fetch(k):
        lanes = pl.ds(pl.multiple_of(k * span, span), span)
        return (
            pltpu.make_async_copy(a_hbm.at[:, lanes], a_ref.at[k], a_sem.at[k]),
            pltpu.make_async_copy(u_hbm.at[:, :, lanes], u_ref.at[k], u_sem.at[k]),
        )

    def give(k):
        lanes = pl.ds(pl.multiple_of(k * span, span), span)
        return pltpu.make_async_copy(l_ref.at[k], l_hbm.at[:, lanes], l_sem.at[k])

    for k in range(chunks):
        for copy in fetch(k):
            copy.start()
    count = k_ref.shape[0] // 2
    local = planes * cells

    dy = line_block(gy_ref, yf_ref, lax.axis_index("row") * cells, cells)
    dz = line_block(gz_ref, zf_ref, lax.axis_index(("chip", "core")) * planes, planes)
    spread_y = (iota((LANES, local), 0) == iota((LANES, local), 1) % cells).astype(F32)
    spread_z = (iota((LANES, local), 0) == iota((LANES, local), 1) // cells).astype(F32)
    dy_tiled = dot(dy, spread_y)
    unit = (iota((cells, local), 0) == iota((cells, local), 1) % cells).astype(F32)
    last = dz[planes - 1 : planes, :] / dz[planes - 1 : planes, planes - 1 : planes]
    first = dz[0:1, :] / dz[0:1, 0:1]
    rows = jnp.concatenate([dz, last, first, jnp.zeros((6, LANES), F32)], axis=0)
    wide = dot(rows, spread_z)
    plane = iota((1, local), 1) // cells

    def unit_part(k, row):
        other = unit * row
        return other + jnp.where(plane == k, dy_tiled, 0.0) if k < planes else other

    for k in range(planes + 2):
        row = wide[k : k + 1, :]
        own, rest = k * cells, count + k * cells
        for lanes, value in ((0, dy_tiled * row), (local, -2.0 * unit_part(k, row))):
            high, low = halves(value)
            k_ref[own : own + cells, lanes : lanes + local] = high
            k_ref[rest : rest + cells, lanes : lanes + local] = low

    def chunk(k, carry):
        for copy in fetch(k):
            copy.wait()
        both = jnp.concatenate(
            [a_ref[k], u_ref[k].reshape(local, span)], axis=0
        )
        high, low = halves(both)
        wide = jnp.dot(k_ref[...], high, preferred_element_type=F32)
        out = wide[:count] + wide[count:]
        out = out + jnp.dot(k_ref[:count], low, preferred_element_type=F32)
        l_ref[k] = out[:local, :]
        zp_ref[:, pl.ds(pl.multiple_of(k * span, span), span)] = out[local:, :]
        give(k).start()
        return carry

    lax.fori_loop(0, chunks, chunk, 0)
    for k in range(chunks):
        give(k).wait()


def reduced_kernel(g_ref, xf_ref, wh_ref, wl_ref, bh_ref, bl_ref, mark_ref):
    groups, width = g_ref.shape[0], g_ref.shape[1]
    order = 2 * groups
    shape = (order, LANES)
    row, col = iota(shape, 0), iota(shape, 1)
    current = ((row == col) | (row + order == col)).astype(F32)
    mark_ref[...] = jnp.zeros_like(mark_ref)
    couple = [half_step * xf_ref[0:1, width * c : width * c + 1] for c in range(1, groups)]
    lane = iota((width, LANES), 1)
    for c in range(groups):
        block = g_ref[c]
        ends = jnp.where(
            lane == 2 * c,
            block[:, 0:1],
            jnp.where(lane == 2 * c + 1, block[:, width - 1 : width], 0.0),
        )
        wh_ref[c, :, :width], wl_ref[c, :, :width] = halves(block)
        wh_ref[c, :, width:], wl_ref[c, :, width:] = halves(ends)
        first_row, last_row = g_ref[c, 0:1, :], g_ref[c, width - 1 : width, :]
        if c > 0:
            at = row == 2 * c - 1
            b = couple[c - 1]
            current = current - jnp.where(at & (col == 2 * c), b * first_row[:, 0:1], 0.0)
            current = current - jnp.where(at & (col == 2 * c + 1), b * last_row[:, 0:1], 0.0)
        if c < groups - 1:
            at = row == 2 * c + 2
            b = couple[c]
            current = current - jnp.where(
                at & (col == 2 * c), b * first_row[:, width - 1 : width], 0.0
            )
            current = current - jnp.where(
                at & (col == 2 * c + 1), b * last_row[:, width - 1 : width], 0.0
            )
    for s in range(order):
        pivot = current[s : s + 1, :] / current[s : s + 1, s : s + 1]
        current = jnp.where(row == s, pivot, current - current[:, s : s + 1] * pivot)
    for c in range(groups):
        span = slice(c * width, (c + 1) * width)
        add = jnp.zeros((order, width), F32)
        if c > 0:
            k = order + 2 * c - 1
            add = add + current[:, k : k + 1] * (couple[c - 1] * g_ref[c, 0:1, :])
        if c < groups - 1:
            k = order + 2 * c + 2
            add = add + current[:, k : k + 1] * (couple[c] * g_ref[c, width - 1 : width, :])
        bh_ref[:, span], bl_ref[:, span] = halves(add)


def dot_halves(both, high, left, right):
    count = high.shape[0]
    wide = jnp.dot(both, left, preferred_element_type=F32)
    return wide[:count] + wide[count:] + jnp.dot(high, right, preferred_element_type=F32)


def x_solve(rows_ref, wh_ref, wl_ref, bh_ref, bl_ref, out_ref, store):
    groups, width = wh_ref.shape[0], wh_ref.shape[1]
    ends = jnp.zeros((rows_ref.shape[0], LANES), F32)
    for c in range(groups):
        at = slice(c * width, (c + 1) * width)
        high, low = halves(rows_ref[:, at])
        wide = dot_halves(jnp.concatenate([high, low], axis=0), high, wh_ref[c], wl_ref[c])
        out_ref[:, at] = wide[:, :width]
        ends = ends + wide[:, width:]
    order = bh_ref.shape[0]
    high, low = halves(ends[:, :order])
    both = jnp.concatenate([high, low], axis=0)
    for c in range(groups // 2):
        at = slice(2 * c * width, 2 * (c + 1) * width)
        store(at, out_ref[:, at] + dot_halves(both, high, bh_ref[:, at], bl_ref[:, at]))


def section_kernel(
    y_ref, zp_ref, gy_ref, yf_ref, gz_ref, zf_ref, keep_ref, send_ref, all_ref
):
    blocks, rows, span = y_ref.shape
    cells = zp_ref.shape[0] // 2
    planes = rows // 4
    mine = lax.axis_index("core")
    dy = line_block(gy_ref, yf_ref, lax.axis_index("row") * cells, cells)
    dz = line_block(gz_ref, zf_ref, lax.axis_index(("chip", "core")) * planes, planes)
    from_last = dy[:, cells - 1 : cells] / dy[cells - 1 : cells, cells - 1 : cells]
    from_first = dy[:, 0:1] / dy[0:1, 0:1]
    last = dz[:, planes - 1 : planes] / dz[planes - 1 : planes, planes - 1 : planes]
    first = dz[:, 0:1] / dz[0:1, 0:1]
    for s in range(blocks):
        at = slice(s * span, (s + 1) * span)
        below = y_ref[s, 0:planes, :]
        above = y_ref[s, 2 * planes : 3 * planes, :]
        for k, w in enumerate((last, first)):
            lo = jnp.sum(w * below, axis=0, keepdims=True)
            hi = jnp.sum(w * above, axis=0, keepdims=True)
            own = slice(k * cells, (k + 1) * cells)
            all_ref[own, at] = zp_ref[own, at] + from_first * lo + from_last * hi
    half = cells // 2
    for k in range(2):
        at = slice(k * half, (k + 1) * half)
        kept = pl.multiple_of(k * cells + mine * half, half)
        sent = pl.multiple_of(k * cells + (1 - mine) * half, half)
        keep_ref[at, :] = all_ref[pl.ds(kept, half), :]
        send_ref[at, :] = all_ref[pl.ds(sent, half), :]


def chip_pair(keep_ref, recv_ref, rows, lanes):
    lower_core = lax.axis_index("core") == 0
    kept, got = keep_ref[rows, lanes], recv_ref[rows, lanes]
    return jnp.where(lower_core, kept, got), jnp.where(lower_core, got, kept)


def pack_kernel(planes, keep_ref, recv_ref, gz_ref, zf_ref, buf_ref, near_ref):
    chip = 2 * planes
    block = line_block(gz_ref, zf_ref, lax.axis_index("chip") * chip, chip)
    e0, e1 = planes - 1, chip - 1
    up = block[e1 : e1 + 1, e0 : e0 + 1] / block[e1 : e1 + 1, e1 : e1 + 1]
    down = block[0:1, planes : planes + 1] / block[0:1, 0:1]
    cross = block[planes : planes + 1, e0 : e0 + 1]
    dests, rows, span = buf_ref.shape
    half = rows // 2
    for d in range(dests):
        lanes = slice(d * span, (d + 1) * span)
        p0, p1 = chip_pair(keep_ref, recv_ref, slice(0, half), lanes)
        buf_ref[d, :half, :] = p1 + up * p0
        near_ref[:half, lanes] = cross * p0
        q0, q1 = chip_pair(keep_ref, recv_ref, slice(half, rows), lanes)
        buf_ref[d, half:, :] = q0 + down * q1
        near_ref[half:, lanes] = cross * q1


def unpack_kernel(planes, back_ref, near_ref, gz_ref, zf_ref, own_ref, sib_ref):
    chip = 2 * planes
    block = line_block(gz_ref, zf_ref, lax.axis_index("chip") * chip, chip)
    e0, b1, e1 = planes - 1, planes, chip - 1
    up = block[b1 : b1 + 1, 0:1] / block[0:1, 0:1]
    down = block[e0 : e0 + 1, e1 : e1 + 1] / block[e1 : e1 + 1, e1 : e1 + 1]
    lower_core = lax.axis_index("core") == 0
    dests, rows, span = back_ref.shape
    half = rows // 2
    for d in range(dests):
        lanes = slice(d * span, (d + 1) * span)
        below0 = back_ref[d, :half, :]
        below1 = up * below0 + near_ref[:half, lanes]
        above1 = back_ref[d, half:, :]
        above0 = down * above1 + near_ref[half:, lanes]
        own_ref[:half, lanes] = jnp.where(lower_core, below0, below1)
        own_ref[half:, lanes] = jnp.where(lower_core, above0, above1)
        sib_ref[:half, lanes] = jnp.where(lower_core, below1, below0)
        sib_ref[half:, lanes] = jnp.where(lower_core, above1, above0)


def inner_kernel(
    l_ref, y_ref, u_ref, gy_ref, yf_ref, gz_ref, zf_ref, wh_ref, wl_ref, bh_ref, bl_ref,
    out_ref, mark_ref, rows_ref, part_ref
):
    mark_ref[...] = jnp.zeros_like(mark_ref)
    blocks, rows, span = y_ref.shape
    planes = rows // 4
    cells = u_ref.shape[1]
    local = planes * cells
    dy = line_block(gy_ref, yf_ref, lax.axis_index("row") * cells, cells)
    dz = line_block(gz_ref, zf_ref, lax.axis_index(("chip", "core")) * planes, planes)
    from_last = dy[:, cells - 1 : cells] / dy[cells - 1 : cells, cells - 1 : cells]
    from_first = dy[:, 0:1] / dy[0:1, 0:1]
    lane = iota((1, LANES), 1)
    parts = []
    for z in range(planes):
        row = jnp.where(lane < planes, dz[z : z + 1, :], jnp.where(lane == planes + z, -2.0, 0.0))
        parts.append(from_first * row + from_last * pltpu.roll(row, 2 * planes, 1))
    mix = jnp.concatenate(parts, axis=0)[:, :rows]
    for s in range(blocks):
        at = slice(s * span, (s + 1) * span)
        rows_ref[:, at] = l_ref[:, at] + dot(mix, y_ref[s])

    def store(at, value):
        for z in range(planes):
            out_ref[z, :, at] = u_ref[z, :, at] + value[z * cells : (z + 1) * cells, :]

    x_solve(rows_ref, wh_ref, wl_ref, bh_ref, bl_ref, part_ref, store)


def final_kernel(
    s_hbm, own_ref, got_ref, gz_ref, zf_ref, wh_ref, wl_ref, bh_ref, bl_ref,
    out_hbm, x_ref, sx_ref, f_ref, in_sem, out_sem
):
    planes, cells = f_ref.shape[0], f_ref.shape[1]
    half = cells // 2

    def fetch(z):
        return pltpu.make_async_copy(s_hbm.at[z], f_ref.at[z], in_sem.at[z])

    def give(z):
        return pltpu.make_async_copy(f_ref.at[z], out_hbm.at[z], out_sem.at[z])

    for z in range(planes):
        fetch(z).start()
    mine = lax.axis_index("core")
    for k in range(2):
        at = slice(k * half, (k + 1) * half)
        own = pl.multiple_of(k * cells + mine * half, half)
        other = pl.multiple_of(k * cells + (1 - mine) * half, half)
        x_ref[pl.ds(own, half), :] = own_ref[at, :]
        x_ref[pl.ds(other, half), :] = got_ref[at, :]
    dz = line_block(gz_ref, zf_ref, lax.axis_index(("chip", "core")) * planes, planes)
    first = dz[:, 0:1] / dz[0:1, 0:1]
    last = dz[:, planes - 1 : planes] / dz[planes - 1 : planes, planes - 1 : planes]

    def store(at, value):
        sx_ref[:, at] = value

    x_solve(x_ref, wh_ref, wl_ref, bh_ref, bl_ref, sx_ref, store)
    for z in range(planes):
        low, high = first[z : z + 1, :], last[z : z + 1, :]
        fetch(z).wait()
        f_ref[z] = f_ref[z] + low * sx_ref[:cells, :] + high * sx_ref[cells:, :]
        give(z).start()
    for z in range(planes):
        give(z).wait()


def body(scalar_field, reaction, x_faces, y_faces, z_faces, x_inverse, y_inverse, z_inverse):
    planes, cells, width = scalar_field.shape
    local = planes * cells
    rows = lax.axis_size("row")
    chips = lax.axis_size("chip")
    xf, yf, zf = x_faces[None, :], y_faces[None, :], z_faces[None, :]
    sds = lambda *s: jax.ShapeDtypeStruct(s, F32)
    held = lambda *s: pltpu.VMEM(s, F32)

    far = pl.BlockSpec(memory_space=pltpu.HBM)
    near_by = pl.BlockSpec(memory_space=pltpu.VMEM)
    field = pltpu.VMEM((planes, cells, width), F32)
    a, y_buf = call(
        explicit_kernel,
        (sds(planes, cells, width), sds(rows, 4 * planes, width // rows)),
        20 * local * width,
        12 * local * width,
        "explicit",
        in_specs=[far] * 5,
        out_specs=(far, near_by),
        scratch_shapes=[
            field,
            field,
            field,
            pltpu.VMEM((1, width), F32),
            pltpu.VMEM((2, 128, 128), F32),
            pltpu.VMEM((1, 256), F32),
            pltpu.VMEM((8, width), F32),
            pltpu.SemaphoreType.DMA((planes,)),
            pltpu.SemaphoreType.DMA((planes,)),
            pltpu.SemaphoreType.DMA((planes,)),
            pltpu.SemaphoreType.DMA((3,)),
        ],
        room=60,
    )(scalar_field, reaction, xf, y_inverse, yf)
    y_in = lax.all_to_all(y_buf, "row", 0, 0, tiled=True)

    y_coef, z_coef = call(coef_kernel, (sds(32, LANES), sds(64, LANES)), 10**8, 10**6, "coefs")(
        y_inverse, yf, z_inverse, zf
    )
    half = lambda *s: jax.ShapeDtypeStruct(s, BF16)
    *weights, x_made = call(
        reduced_kernel,
        (
            half(16, 128, 256),
            half(16, 128, 256),
            half(32, width),
            half(32, width),
            held(8, LANES),
        ),
        10**9,
        2 * 10**6,
        "reduced",
        room=60,
    )(x_inverse, xf)
    chunks = 4
    field_chunks = pltpu.VMEM((chunks, planes, cells, width // chunks), F32)
    inside, z_part = call(
        local_kernel,
        (sds(local, width), held(2 * cells, width)),
        6 * 320 * 512 * width,
        14 * local * width,
        "local",
        in_specs=[far, far] + [near_by] * 4,
        out_specs=(far, near_by),
        scratch_shapes=[
            pltpu.VMEM((2 * (local + 2 * cells), 2 * local), BF16),
            pltpu.VMEM((chunks, local, width // chunks), F32),
            field_chunks,
            pltpu.VMEM((chunks, local, width // chunks), F32),
            pltpu.SemaphoreType.DMA((chunks,)),
            pltpu.SemaphoreType.DMA((chunks,)),
            pltpu.SemaphoreType.DMA((chunks,)),
        ],
        input_output_aliases={0: 0},
        room=61.5,
    )(a.reshape(local, width), scalar_field, y_inverse, yf, z_inverse, zf)

    y_out = call(scan_kernel, sds(*y_in.shape), 10**6, 10**6, "scan_y")(y_in, y_coef)
    y_back = lax.all_to_all(y_out, "row", 0, 0, tiled=True)

    keep, send = call(
        section_kernel,
        (sds(cells, width), sds(cells, width)),
        10**7,
        10**6,
        "section",
        scratch_shapes=[pltpu.VMEM((2 * cells, width), F32)],
    )(y_back, z_part, y_inverse, yf, z_inverse, zf)
    pairs = [(0, 1), (1, 0)]
    recv = lax.ppermute(send, "core", pairs)
    z_buf, near = call(
        functools.partial(pack_kernel, planes),
        (sds(chips, cells, width // chips), sds(cells, width)),
        10**6,
        10**6,
        "pack",
    )(keep, recv, z_inverse, zf)
    z_in = lax.all_to_all(z_buf, "chip", 0, 0, tiled=True)

    z_out = call_after(
        (x_made,), scan_kernel, sds(*z_in.shape), 10**6, 10**6, "scan_z", z_in, z_coef
    )
    z_back = lax.all_to_all(z_out, "chip", 0, 0, tiled=True)
    partial_out, inner_made = call(
        inner_kernel,
        (sds(planes, cells, width), held(8, LANES)),
        12 * local * width * 200,
        16 * local * width,
        "inner",
        scratch_shapes=[pltpu.VMEM((local, width), F32), pltpu.VMEM((local, width), F32)],
        room=60,
    )(inside, y_back, scalar_field, y_inverse, yf, z_inverse, zf, *weights)
    own, sib = call_after(
        (inner_made,),
        functools.partial(unpack_kernel, planes),
        (sds(cells, width), sds(cells, width)),
        10**6,
        10**6,
        "unpack",
        z_back,
        near,
        z_inverse,
        zf,
    )
    got = lax.ppermute(sib, "core", pairs)
    return call(
        final_kernel,
        sds(planes, cells, width),
        12 * local * width,
        8 * local * width,
        "final",
        in_specs=[far] + [near_by] * 8,
        out_specs=far,
        scratch_shapes=[
            pltpu.VMEM((2 * cells, width), F32),
            pltpu.VMEM((2 * cells, width), F32),
            field,
            pltpu.SemaphoreType.DMA((planes,)),
            pltpu.SemaphoreType.DMA((planes,)),
        ],
        input_output_aliases={0: 0},
    )(partial_out, own, got, z_inverse, zf, *weights)


def solution(mesh):
    rows, columns = mesh.shape["row"], mesh.shape["col"]
    split = Mesh(mesh.devices.reshape(rows, columns // 2, 2), ("row", "chip", "core"))
    field = P(("chip", "core"), "row", None)
    in_specs = (field, field, P(), P(), P(), P(), P(), P())
    return jax.shard_map(body, mesh=split, in_specs=in_specs, out_specs=field, check_vma=False)
```

```python
import functools

import jax
import jax.numpy as jnp
from jax import lax
from jax.experimental import pallas as pl
from jax.experimental.pallas import tpu as pltpu
from jax.sharding import Mesh
from jax.sharding import PartitionSpec as P

F32 = jnp.float32
BF16 = jnp.bfloat16
half_step = 500.0
time_step = 1000.0
LANES = 128


def dot(left, right):
    return lax.dot_general(
        left,
        right,
        (((1,), (0,)), ((), ())),
        precision=lax.Precision.HIGHEST,
        preferred_element_type=F32,
    )


def halves(value):
    high = value.astype(BF16)
    return high, (value - high.astype(F32)).astype(BF16)


def iota(shape, dim):
    return lax.broadcasted_iota(jnp.int32, shape, dim)


def joint(g_ref, faces_ref):
    b = half_step * faces_ref[0:1, 128:129]
    g0 = g_ref[0, 127:128, 127:128]
    g1 = g_ref[1, 0:1, 0:1]
    den = 1.0 - b * b * g0 * g1
    return b * b * g1 / den, b * b * g0 / den, b / den


def line_block(g_ref, faces_ref, start, size):
    alpha0, alpha1, _ = joint(g_ref, faces_ref)
    group = start // 128
    offset = start - group * 128
    rows = g_ref[group, pl.ds(pl.multiple_of(offset, size), size), :]
    low = group == 0
    edge_row = jnp.where(low, g_ref[0, 127:128, :], g_ref[1, 0:1, :])
    edge_col = jnp.where(low, rows[:, 127:128], rows[:, 0:1])
    alpha = jnp.where(low, alpha0, alpha1)
    block = rows + (alpha * edge_col) * edge_row
    return pltpu.roll(block, lax.rem(128 - offset, 128), 1)


def element(g_ref, joined, i, j):
    alpha0, alpha1, beta = joined
    gi, gj = i // 128, j // 128
    li, lj = i % 128, j % 128
    ei, ej = (0 if gi else 127), (0 if gj else 127)
    across = g_ref[gi, li : li + 1, ei : ei + 1] * g_ref[gj, ej : ej + 1, lj : lj + 1]
    if gi == gj:
        alpha = alpha1 if gi else alpha0
        return g_ref[gi, li : li + 1, lj : lj + 1] + alpha * across
    return beta * across


MIB = 1024 * 1024


def call(kernel, out_shape, flops, nbytes, name, room=20, **kw):
    return pl.pallas_call(
        kernel,
        out_shape=out_shape,
        name=name,
        compiler_params=pltpu.CompilerParams(vmem_limit_bytes=int(room * MIB)),
        cost_estimate=pl.CostEstimate(flops=flops, bytes_accessed=nbytes, transcendentals=0),
        **kw,
    )


def call_after(earlier, kernel, out_shape, flops, nbytes, name, *args, **kw):
    count, extra = len(args), len(earlier)

    def ordered(*refs):
        kernel(*refs[:count], *refs[count + extra :])

    specs = [pl.BlockSpec(memory_space=pltpu.VMEM)] * count + [pl.BlockSpec(memory_space=pltpu.HBM)] * extra
    return call(ordered, out_shape, flops, nbytes, name, in_specs=specs, **kw)(*args, *earlier)


def explicit_kernel(
    u_hbm, r_hbm, xf_hbm, gy_hbm, yf_hbm, a_hbm, ends_ref,
    buf_ref, u_ref, r_ref, a_ref, xf_ref, gy_ref, yf_ref, f_ref, u_sem, r_sem, a_sem, s_sem
):
    planes, cells, width = u_ref.shape
    small = [
        pltpu.make_async_copy(gy_hbm, gy_ref, s_sem.at[0]),
        pltpu.make_async_copy(yf_hbm, yf_ref, s_sem.at[1]),
        pltpu.make_async_copy(xf_hbm, xf_ref, s_sem.at[2]),
    ]
    for copy in small:
        copy.start()

    def fetch(z):
        return (
            pltpu.make_async_copy(u_hbm.at[z], u_ref.at[z], u_sem.at[z]),
            pltpu.make_async_copy(r_hbm.at[z], r_ref.at[z], r_sem.at[z]),
        )

    def give(z):
        return pltpu.make_async_copy(a_ref.at[z], a_hbm.at[z], a_sem.at[z])

    for z in range(planes):
        for copy in fetch(z):
            copy.start()
    for copy in small:
        copy.wait()

    block = line_block(gy_ref, yf_ref, lax.axis_index("row") * cells, cells)
    last = block[:, cells - 1 : cells] / block[cells - 1 : cells, cells - 1 : cells]
    first = block[:, 0:1] / block[0:1, 0:1]
    w = [jnp.broadcast_to(v, (cells, LANES)) for v in (last, first)]
    here = time_step * xf_ref[...]
    lane = iota((1, width), 1)
    after = jnp.where(lane == width - 1, 0.0, pltpu.roll(here, width - 1, 1))
    f_ref[0:1, :] = after
    f_ref[1:2, :] = jnp.where(lane == 0, 0.0, here)
    f_ref[2:3, :] = 4.0 - (after + here)

    span = buf_ref.shape[2]
    count = width // LANES
    lane = iota((cells, LANES), 1)

    def plane(z, carry):
        for copy in fetch(z):
            copy.wait()

        def column(c):
            here = u_ref[z, :, c * LANES : (c + 1) * LANES]
            return here, pltpu.roll(here, 1, 1), pltpu.roll(here, LANES - 1, 1)

        sums = {}
        before = jnp.zeros((cells, LANES), F32)
        now = column(0)
        for c in range(count):
            then = column(c + 1) if c + 1 < count else (None, None, before)
            u = now[0]
            lower = jnp.where(lane == 0, before, now[1])
            upper = jnp.where(lane == LANES - 1, then[2], now[2])
            at = slice(c * LANES, (c + 1) * LANES)
            rate = r_ref[z, :, at] * (time_step - time_step * (u * u)) + f_ref[2:3, at]
            a = f_ref[0:1, at] * upper + f_ref[1:2, at] * lower + rate * u
            a_ref[z, :, at] = a
            for k in range(2):
                for f, field in enumerate((a, u)):
                    row = jnp.sum(w[k] * field, axis=0, keepdims=True)
                    sums.setdefault((k, f), []).append(row)
            if (c + 1) * LANES % span == 0:
                for (k, f), pieces in sums.items():
                    row = jnp.concatenate(pieces, axis=1)
                    buf_ref[c * LANES // span, pl.ds(z + 16 * k + 8 * f, 1), :] = row
                sums = {}
            before, now = now[1], then
        give(z).start()
        return carry

    lax.fori_loop(0, planes, plane, 0)
    for d in range(width // span):
        ends_ref[:, d * span : (d + 1) * span] = buf_ref[d]
    for z in range(planes):
        give(z).wait()


def coef_kernel(count, g_ref, f_ref, out_ref):
    joined = joint(g_ref, f_ref)
    size = 256 // count
    m = functools.partial(element, g_ref, joined)
    out_ref[...] = jnp.zeros_like(out_ref)
    for c in range(count):
        b, e = c * size, c * size + size - 1
        if c > 0:
            ee = m(e, e - size) / m(e, e)
            be = m(b, b - 1)
            out_ref[c : c + 1, :] = jnp.broadcast_to(ee, (1, LANES))
            out_ref[count + c : count + c + 1, :] = jnp.broadcast_to(be, (1, LANES))
        if c < count - 1:
            bb = m(b, b + size) / m(b, b)
            eb = m(e, e + 1)
            out_ref[2 * count + c : 2 * count + c + 1, :] = jnp.broadcast_to(bb, (1, LANES))
            out_ref[3 * count + c : 3 * count + c + 1, :] = jnp.broadcast_to(eb, (1, LANES))


def line_rows(g_ref, faces_ref, start, size):
    alpha0, alpha1, beta = joint(g_ref, faces_ref)
    group = start // 128
    offset = start - group * 128
    rows = g_ref[group, pl.ds(pl.multiple_of(offset, size), size), :]
    low = group == 0
    edge = jnp.where(low, rows[:, 127:128], rows[:, 0:1])
    end0, end1 = g_ref[0, 127:128, :], g_ref[1, 0:1, :]
    left = jnp.where(low, rows + (alpha0 * edge) * end0, (beta * edge) * end0)
    right = jnp.where(low, (beta * edge) * end1, rows + (alpha1 * edge) * end1)
    return left, right


def pair_kernel(cells, rings, mine_ref, got_ref, gy_ref, yf_ref, *out_refs):
    *send_refs, near_ref = out_refs
    r = lax.axis_index("row")
    pair = r // 2
    lower = r % 2 == 0
    block = line_block(gy_ref, yf_ref, pair * (2 * cells), 2 * cells)
    e0, b1, e1 = cells - 1, cells, 2 * cells - 1
    up = block[e1 : e1 + 1, e0 : e0 + 1] / block[e1 : e1 + 1, e1 : e1 + 1]
    down = block[0:1, b1 : b1 + 1] / block[0:1, 0:1]
    cross = block[b1 : b1 + 1, e0 : e0 + 1]
    half = mine_ref.shape[0] // 2
    span = 512
    for s in range(mine_ref.shape[1] // span):
        at = slice(s * span, (s + 1) * span)
        p, p_got = mine_ref[:half, at], got_ref[:half, at]
        q, q_got = mine_ref[half:, at], got_ref[half:, at]
        p0, p1 = jnp.where(lower, p, p_got), jnp.where(lower, p_got, p)
        q0, q1 = jnp.where(lower, q, q_got), jnp.where(lower, q_got, q)
        below = p1 + up * p0
        above = q0 + down * q1
        for k, send_ref in enumerate(send_refs):
            send_ref[:, at] = jnp.where(pair + k + 1 < rings, below, above)
        near_ref[:half, at] = jnp.where(lower, 0.0, cross * p0)
        near_ref[half:, at] = jnp.where(lower, cross * q1, 0.0)


def scan_kernel(in_ref, c_ref, out_ref):
    count, rows, span = in_ref.shape
    half = rows // 2

    def coef(k):
        return c_ref[k : k + 1, 0:1]

    zero = jnp.zeros((half, span), F32)
    out_ref[0, :half, :] = zero
    out_ref[count - 1, half:, :] = zero
    below = above = None
    for s in range(count - 1):
        own = in_ref[s, :half, :]
        below = own if s == 0 else own + coef(s) * below
        out_ref[s + 1, :half, :] = coef(count + s + 1) * below
        t = count - 1 - s
        own = in_ref[t, half:, :]
        above = own if s == 0 else own + coef(2 * count + t) * above
        out_ref[t - 1, half:, :] = coef(3 * count + t - 1) * above


def local_kernel(
    a_hbm, u_hbm, gy_ref, yf_ref, gz_ref, zf_ref, l_hbm, zp_ref,
    k_ref, a_ref, u_ref, l_ref, a_sem, u_sem, l_sem
):
    chunks, planes, cells, span = u_ref.shape

    def fetch(k):
        lanes = pl.ds(pl.multiple_of(k * span, span), span)
        return (
            pltpu.make_async_copy(a_hbm.at[:, lanes], a_ref.at[k], a_sem.at[k]),
            pltpu.make_async_copy(u_hbm.at[:, :, lanes], u_ref.at[k], u_sem.at[k]),
        )

    def give(k):
        lanes = pl.ds(pl.multiple_of(k * span, span), span)
        return pltpu.make_async_copy(l_ref.at[k], l_hbm.at[:, lanes], l_sem.at[k])

    for k in range(chunks):
        for copy in fetch(k):
            copy.start()
    count = k_ref.shape[0] // 2
    local = planes * cells

    dy = line_block(gy_ref, yf_ref, lax.axis_index("row") * cells, cells)
    dz = line_block(gz_ref, zf_ref, lax.axis_index(("chip", "core")) * planes, planes)
    spread_y = (iota((LANES, local), 0) == iota((LANES, local), 1) % cells).astype(F32)
    spread_z = (iota((LANES, local), 0) == iota((LANES, local), 1) // cells).astype(F32)
    dy_tiled = dot(dy, spread_y)
    unit = (iota((cells, local), 0) == iota((cells, local), 1) % cells).astype(F32)
    last = dz[planes - 1 : planes, :] / dz[planes - 1 : planes, planes - 1 : planes]
    first = dz[0:1, :] / dz[0:1, 0:1]
    rows = jnp.concatenate([dz, last, first, jnp.zeros((6, LANES), F32)], axis=0)
    wide = dot(rows, spread_z)
    plane = iota((1, local), 1) // cells

    def unit_part(k, row):
        other = unit * row
        return other + jnp.where(plane == k, dy_tiled, 0.0) if k < planes else other

    for k in range(planes + 2):
        row = wide[k : k + 1, :]
        own, rest = k * cells, count + k * cells
        for lanes, value in ((0, dy_tiled * row), (local, -2.0 * unit_part(k, row))):
            high, low = halves(value)
            k_ref[own : own + cells, lanes : lanes + local] = high
            k_ref[rest : rest + cells, lanes : lanes + local] = low

    def chunk(k, carry):
        for copy in fetch(k):
            copy.wait()
        both = jnp.concatenate(
            [a_ref[k], u_ref[k].reshape(local, span)], axis=0
        )
        high, low = halves(both)
        wide = jnp.dot(k_ref[...], high, preferred_element_type=F32)
        out = wide[:count] + wide[count:]
        out = out + jnp.dot(k_ref[:count], low, preferred_element_type=F32)
        l_ref[k] = out[:local, :]
        zp_ref[:, pl.ds(pl.multiple_of(k * span, span), span)] = out[local:, :]
        give(k).start()
        return carry

    lax.fori_loop(0, chunks, chunk, 0)
    for k in range(chunks):
        give(k).wait()


def reduced_kernel(g_ref, xf_ref, wh_ref, wl_ref, bh_ref, bl_ref, mark_ref):
    groups, width = g_ref.shape[0], g_ref.shape[1]
    order = 2 * groups
    shape = (order, LANES)
    row, col = iota(shape, 0), iota(shape, 1)
    current = ((row == col) | (row + order == col)).astype(F32)
    mark_ref[...] = jnp.zeros_like(mark_ref)
    couple = [half_step * xf_ref[0:1, width * c : width * c + 1] for c in range(1, groups)]
    lane = iota((width, LANES), 1)
    for c in range(groups):
        block = g_ref[c]
        ends = jnp.where(
            lane == 2 * c,
            block[:, 0:1],
            jnp.where(lane == 2 * c + 1, block[:, width - 1 : width], 0.0),
        )
        wh_ref[c, :, :width], wl_ref[c, :, :width] = halves(block)
        wh_ref[c, :, width:], wl_ref[c, :, width:] = halves(ends)
        first_row, last_row = g_ref[c, 0:1, :], g_ref[c, width - 1 : width, :]
        if c > 0:
            at = row == 2 * c - 1
            b = couple[c - 1]
            current = current - jnp.where(at & (col == 2 * c), b * first_row[:, 0:1], 0.0)
            current = current - jnp.where(at & (col == 2 * c + 1), b * last_row[:, 0:1], 0.0)
        if c < groups - 1:
            at = row == 2 * c + 2
            b = couple[c]
            current = current - jnp.where(
                at & (col == 2 * c), b * first_row[:, width - 1 : width], 0.0
            )
            current = current - jnp.where(
                at & (col == 2 * c + 1), b * last_row[:, width - 1 : width], 0.0
            )
    for s in range(order):
        pivot = current[s : s + 1, :] / current[s : s + 1, s : s + 1]
        current = jnp.where(row == s, pivot, current - current[:, s : s + 1] * pivot)
    for c in range(groups):
        span = slice(c * width, (c + 1) * width)
        add = jnp.zeros((order, width), F32)
        if c > 0:
            k = order + 2 * c - 1
            add = add + current[:, k : k + 1] * (couple[c - 1] * g_ref[c, 0:1, :])
        if c < groups - 1:
            k = order + 2 * c + 2
            add = add + current[:, k : k + 1] * (couple[c] * g_ref[c, width - 1 : width, :])
        bh_ref[:, span], bl_ref[:, span] = halves(add)


def dot_halves(both, high, left, right):
    count = high.shape[0]
    wide = jnp.dot(both, left, preferred_element_type=F32)
    return wide[:count] + wide[count:] + jnp.dot(high, right, preferred_element_type=F32)


def x_solve(rows_ref, wh_ref, wl_ref, bh_ref, bl_ref, out_ref, store):
    groups, width = wh_ref.shape[0], wh_ref.shape[1]
    ends = jnp.zeros((rows_ref.shape[0], LANES), F32)
    for c in range(groups):
        at = slice(c * width, (c + 1) * width)
        high, low = halves(rows_ref[:, at])
        wide = dot_halves(jnp.concatenate([high, low], axis=0), high, wh_ref[c], wl_ref[c])
        out_ref[:, at] = wide[:, :width]
        ends = ends + wide[:, width:]
    order = bh_ref.shape[0]
    high, low = halves(ends[:, :order])
    both = jnp.concatenate([high, low], axis=0)
    for c in range(groups // 2):
        at = slice(2 * c * width, 2 * (c + 1) * width)
        store(at, out_ref[:, at] + dot_halves(both, high, bh_ref[:, at], bl_ref[:, at]))


def section_kernel(
    near_ref, r1_ref, r2_ref, r3_ref, zp_ref, gy_ref, yf_ref, gz_ref, zf_ref,
    keep_ref, send_ref, rows_ref, all_ref
):
    rows, width = near_ref.shape
    cells = zp_ref.shape[0] // 2
    planes = rows // 4
    mine = lax.axis_index("core")
    r = lax.axis_index("row")
    pair = r // 2
    dy = line_block(gy_ref, yf_ref, r * cells, cells)
    dz = line_block(gz_ref, zf_ref, lax.axis_index(("chip", "core")) * planes, planes)
    from_last = dy[:, cells - 1 : cells] / dy[cells - 1 : cells, cells - 1 : cells]
    from_first = dy[:, 0:1] / dy[0:1, 0:1]
    last = dz[:, planes - 1 : planes] / dz[planes - 1 : planes, planes - 1 : planes]
    first = dz[:, 0:1] / dz[0:1, 0:1]
    full = line_rows(gy_ref, yf_ref, r * cells, cells)
    step = 2 * cells
    below, above = [], []
    for k in range(1, 4):
        lo = hi = jnp.zeros((1, 1), F32)
        for t in range(4):
            b, e = t * step % 128, t * step % 128 + step - 1
            part = full[t * step // 128]
            lo = jnp.where(pair - k == t, part[0:1, e : e + 1], lo)
            hi = jnp.where(pair - k + 4 == t, part[cells - 1 : cells, b : b + 1], hi)
        below.append(lo)
        above.append(hi)
    half = rows // 2
    span = 256
    for s in range(width // span):
        at = slice(s * span, (s + 1) * span)
        got = [ref[:, at] for ref in (r1_ref, r2_ref, r3_ref)]
        lo = near_ref[:half, at] + sum(c * g for c, g in zip(below, got))
        hi = near_ref[half:, at] + sum(c * g for c, g in zip(above, got))
        rows_ref[:half, at] = lo
        rows_ref[half:, at] = hi
        for k, w in enumerate((last, first)):
            low = jnp.sum(w * lo[:planes], axis=0, keepdims=True)
            high = jnp.sum(w * hi[:planes], axis=0, keepdims=True)
            own = slice(k * cells, (k + 1) * cells)
            all_ref[own, at] = zp_ref[own, at] + from_first * low + from_last * high
    half = cells // 2
    for k in range(2):
        at = slice(k * half, (k + 1) * half)
        kept = pl.multiple_of(k * cells + mine * half, half)
        sent = pl.multiple_of(k * cells + (1 - mine) * half, half)
        keep_ref[at, :] = all_ref[pl.ds(kept, half), :]
        send_ref[at, :] = all_ref[pl.ds(sent, half), :]


def chip_pair(keep_ref, recv_ref, rows, lanes):
    lower_core = lax.axis_index("core") == 0
    kept, got = keep_ref[rows, lanes], recv_ref[rows, lanes]
    return jnp.where(lower_core, kept, got), jnp.where(lower_core, got, kept)


def pack_kernel(planes, keep_ref, recv_ref, gz_ref, zf_ref, buf_ref, near_ref):
    chip = 2 * planes
    block = line_block(gz_ref, zf_ref, lax.axis_index("chip") * chip, chip)
    e0, e1 = planes - 1, chip - 1
    up = block[e1 : e1 + 1, e0 : e0 + 1] / block[e1 : e1 + 1, e1 : e1 + 1]
    down = block[0:1, planes : planes + 1] / block[0:1, 0:1]
    cross = block[planes : planes + 1, e0 : e0 + 1]
    dests, rows, span = buf_ref.shape
    half = rows // 2
    for d in range(dests):
        lanes = slice(d * span, (d + 1) * span)
        p0, p1 = chip_pair(keep_ref, recv_ref, slice(0, half), lanes)
        buf_ref[d, :half, :] = p1 + up * p0
        near_ref[:half, lanes] = cross * p0
        q0, q1 = chip_pair(keep_ref, recv_ref, slice(half, rows), lanes)
        buf_ref[d, half:, :] = q0 + down * q1
        near_ref[half:, lanes] = cross * q1


def unpack_kernel(planes, back_ref, near_ref, gz_ref, zf_ref, own_ref, sib_ref):
    chip = 2 * planes
    block = line_block(gz_ref, zf_ref, lax.axis_index("chip") * chip, chip)
    e0, b1, e1 = planes - 1, planes, chip - 1
    up = block[b1 : b1 + 1, 0:1] / block[0:1, 0:1]
    down = block[e0 : e0 + 1, e1 : e1 + 1] / block[e1 : e1 + 1, e1 : e1 + 1]
    lower_core = lax.axis_index("core") == 0
    dests, rows, span = back_ref.shape
    half = rows // 2
    for d in range(dests):
        lanes = slice(d * span, (d + 1) * span)
        below0 = back_ref[d, :half, :]
        below1 = up * below0 + near_ref[:half, lanes]
        above1 = back_ref[d, half:, :]
        above0 = down * above1 + near_ref[half:, lanes]
        own_ref[:half, lanes] = jnp.where(lower_core, below0, below1)
        own_ref[half:, lanes] = jnp.where(lower_core, above0, above1)
        sib_ref[:half, lanes] = jnp.where(lower_core, below1, below0)
        sib_ref[half:, lanes] = jnp.where(lower_core, above1, above0)


def inner_kernel(
    l_ref, y_ref, u_ref, gy_ref, yf_ref, gz_ref, zf_ref, wh_ref, wl_ref, bh_ref, bl_ref,
    out_ref, mark_ref, rows_ref, part_ref
):
    mark_ref[...] = jnp.zeros_like(mark_ref)
    rows, width = y_ref.shape
    planes = rows // 4
    cells = u_ref.shape[1]
    local = planes * cells
    dy = line_block(gy_ref, yf_ref, lax.axis_index("row") * cells, cells)
    dz = line_block(gz_ref, zf_ref, lax.axis_index(("chip", "core")) * planes, planes)
    from_last = dy[:, cells - 1 : cells] / dy[cells - 1 : cells, cells - 1 : cells]
    from_first = dy[:, 0:1] / dy[0:1, 0:1]
    lane = iota((1, LANES), 1)
    parts = []
    for z in range(planes):
        row = jnp.where(lane < planes, dz[z : z + 1, :], jnp.where(lane == planes + z, -2.0, 0.0))
        parts.append(from_first * row + from_last * pltpu.roll(row, 2 * planes, 1))
    mix = jnp.concatenate(parts, axis=0)[:, :rows]
    span = 256
    for s in range(width // span):
        at = slice(s * span, (s + 1) * span)
        rows_ref[:, at] = l_ref[:, at] + dot(mix, y_ref[:, at])

    def store(at, value):
        for z in range(planes):
            out_ref[z, :, at] = u_ref[z, :, at] + value[z * cells : (z + 1) * cells, :]

    x_solve(rows_ref, wh_ref, wl_ref, bh_ref, bl_ref, part_ref, store)


def final_kernel(
    s_hbm, own_ref, got_ref, gz_ref, zf_ref, wh_ref, wl_ref, bh_ref, bl_ref,
    out_hbm, x_ref, sx_ref, f_ref, in_sem, out_sem
):
    planes, cells = f_ref.shape[0], f_ref.shape[1]
    half = cells // 2

    def fetch(z):
        return pltpu.make_async_copy(s_hbm.at[z], f_ref.at[z], in_sem.at[z])

    def give(z):
        return pltpu.make_async_copy(f_ref.at[z], out_hbm.at[z], out_sem.at[z])

    for z in range(planes):
        fetch(z).start()
    mine = lax.axis_index("core")
    for k in range(2):
        at = slice(k * half, (k + 1) * half)
        own = pl.multiple_of(k * cells + mine * half, half)
        other = pl.multiple_of(k * cells + (1 - mine) * half, half)
        x_ref[pl.ds(own, half), :] = own_ref[at, :]
        x_ref[pl.ds(other, half), :] = got_ref[at, :]
    dz = line_block(gz_ref, zf_ref, lax.axis_index(("chip", "core")) * planes, planes)
    first = dz[:, 0:1] / dz[0:1, 0:1]
    last = dz[:, planes - 1 : planes] / dz[planes - 1 : planes, planes - 1 : planes]

    def store(at, value):
        sx_ref[:, at] = value

    x_solve(x_ref, wh_ref, wl_ref, bh_ref, bl_ref, sx_ref, store)
    for z in range(planes):
        low, high = first[z : z + 1, :], last[z : z + 1, :]
        fetch(z).wait()
        f_ref[z] = f_ref[z] + low * sx_ref[:cells, :] + high * sx_ref[cells:, :]
        give(z).start()
    for z in range(planes):
        give(z).wait()


def body(scalar_field, reaction, x_faces, y_faces, z_faces, x_inverse, y_inverse, z_inverse):
    planes, cells, width = scalar_field.shape
    local = planes * cells
    rows = lax.axis_size("row")
    chips = lax.axis_size("chip")
    xf, yf, zf = x_faces[None, :], y_faces[None, :], z_faces[None, :]
    sds = lambda *s: jax.ShapeDtypeStruct(s, F32)
    held = lambda *s: pltpu.VMEM(s, F32)

    far = pl.BlockSpec(memory_space=pltpu.HBM)
    near_by = pl.BlockSpec(memory_space=pltpu.VMEM)
    field = pltpu.VMEM((planes, cells, width), F32)
    a, ends = call(
        explicit_kernel,
        (sds(planes, cells, width), held(4 * planes, width)),
        20 * local * width,
        12 * local * width,
        "explicit",
        in_specs=[far] * 5,
        out_specs=(far, near_by),
        scratch_shapes=[
            pltpu.VMEM((8, 4 * planes, width // 8), F32),
            field,
            field,
            field,
            pltpu.VMEM((1, width), F32),
            pltpu.VMEM((2, 128, 128), F32),
            pltpu.VMEM((1, 256), F32),
            pltpu.VMEM((8, width), F32),
            pltpu.SemaphoreType.DMA((planes,)),
            pltpu.SemaphoreType.DMA((planes,)),
            pltpu.SemaphoreType.DMA((planes,)),
            pltpu.SemaphoreType.DMA((3,)),
        ],
        room=60,
    )(scalar_field, reaction, xf, y_inverse, yf)
    got_ends = lax.ppermute(ends, "row", [(i, i ^ 1) for i in range(rows)])

    z_coef = call(
        functools.partial(coef_kernel, chips), held(4 * chips, LANES), 10**8, 10**6, "coefs"
    )(z_inverse, zf)
    half = lambda *s: jax.ShapeDtypeStruct(s, BF16)
    *weights, x_made = call(
        reduced_kernel,
        (
            half(16, 128, 256),
            half(16, 128, 256),
            half(32, width),
            half(32, width),
            held(8, LANES),
        ),
        10**9,
        2 * 10**6,
        "reduced",
        room=60,
    )(x_inverse, xf)
    chunks = 4
    field_chunks = pltpu.VMEM((chunks, planes, cells, width // chunks), F32)
    inside, z_part = call(
        local_kernel,
        (sds(local, width), held(2 * cells, width)),
        6 * 320 * 512 * width,
        14 * local * width,
        "local",
        in_specs=[far, far] + [near_by] * 4,
        out_specs=(far, near_by),
        scratch_shapes=[
            pltpu.VMEM((2 * (local + 2 * cells), 2 * local), BF16),
            pltpu.VMEM((chunks, local, width // chunks), F32),
            field_chunks,
            pltpu.VMEM((chunks, local, width // chunks), F32),
            pltpu.SemaphoreType.DMA((chunks,)),
            pltpu.SemaphoreType.DMA((chunks,)),
            pltpu.SemaphoreType.DMA((chunks,)),
        ],
        input_output_aliases={0: 0},
        room=61.5,
    )(a.reshape(local, width), scalar_field, y_inverse, yf, z_inverse, zf)

    *sums, near_y = call_after(
        (z_coef,),
        functools.partial(pair_kernel, cells, rows // 2),
        tuple(sds(2 * planes, width) for _ in range(3)) + (sds(4 * planes, width),),
        10**6,
        10**6,
        "pair",
        ends,
        got_ends,
        y_inverse,
        yf,
    )
    got_sums = [
        lax.ppermute(total, "row", [(i, (i + 2 * k + 2) % rows) for i in range(rows)])
        for k, total in enumerate(sums)
    ]

    keep, send, y_rows = call(
        section_kernel,
        (sds(cells, width), sds(cells, width), sds(4 * planes, width)),
        10**7,
        10**6,
        "section",
        scratch_shapes=[pltpu.VMEM((2 * cells, width), F32)],
    )(near_y, *got_sums, z_part, y_inverse, yf, z_inverse, zf)
    pairs = [(0, 1), (1, 0)]
    recv = lax.ppermute(send, "core", pairs)
    z_buf, near = call(
        functools.partial(pack_kernel, planes),
        (sds(chips, cells, width // chips), sds(cells, width)),
        10**6,
        10**6,
        "pack",
    )(keep, recv, z_inverse, zf)
    z_in = lax.all_to_all(z_buf, "chip", 0, 0, tiled=True)

    z_out = call_after(
        (x_made,), scan_kernel, sds(*z_in.shape), 10**6, 10**6, "scan_z", z_in, z_coef
    )
    z_back = lax.all_to_all(z_out, "chip", 0, 0, tiled=True)
    partial_out, inner_made = call(
        inner_kernel,
        (sds(planes, cells, width), held(8, LANES)),
        12 * local * width * 200,
        16 * local * width,
        "inner",
        scratch_shapes=[pltpu.VMEM((local, width), F32), pltpu.VMEM((local, width), F32)],
        room=60,
    )(inside, y_rows, scalar_field, y_inverse, yf, z_inverse, zf, *weights)
    own, sib = call_after(
        (inner_made,),
        functools.partial(unpack_kernel, planes),
        (sds(cells, width), sds(cells, width)),
        10**6,
        10**6,
        "unpack",
        z_back,
        near,
        z_inverse,
        zf,
    )
    got = lax.ppermute(sib, "core", pairs)
    return call(
        final_kernel,
        sds(planes, cells, width),
        12 * local * width,
        8 * local * width,
        "final",
        in_specs=[far] + [near_by] * 8,
        out_specs=far,
        scratch_shapes=[
            pltpu.VMEM((2 * cells, width), F32),
            pltpu.VMEM((2 * cells, width), F32),
            field,
            pltpu.SemaphoreType.DMA((planes,)),
            pltpu.SemaphoreType.DMA((planes,)),
        ],
        input_output_aliases={0: 0},
    )(partial_out, own, got, z_inverse, zf, *weights)


def solution(mesh):
    rows, columns = mesh.shape["row"], mesh.shape["col"]
    split = Mesh(mesh.devices.reshape(rows, columns // 2, 2), ("row", "chip", "core"))
    field = P(("chip", "core"), "row", None)
    in_specs = (field, field, P(), P(), P(), P(), P(), P())
    return jax.shard_map(body, mesh=split, in_specs=in_specs, out_specs=field, check_vma=False)
```

```python
import functools

import jax
import jax.numpy as jnp
from jax import lax
from jax.experimental import pallas as pl
from jax.experimental.pallas import tpu as pltpu
from jax.sharding import Mesh
from jax.sharding import PartitionSpec as P

F32 = jnp.float32
BF16 = jnp.bfloat16
half_step = 500.0
time_step = 1000.0
LANES = 128


def dot(left, right):
    return lax.dot_general(
        left,
        right,
        (((1,), (0,)), ((), ())),
        precision=lax.Precision.HIGHEST,
        preferred_element_type=F32,
    )


def halves(value):
    high = value.astype(BF16)
    return high, (value - high.astype(F32)).astype(BF16)


def iota(shape, dim):
    return lax.broadcasted_iota(jnp.int32, shape, dim)


def joint(g_ref, faces_ref):
    b = half_step * faces_ref[0:1, 128:129]
    g0 = g_ref[0, 127:128, 127:128]
    g1 = g_ref[1, 0:1, 0:1]
    den = 1.0 - b * b * g0 * g1
    return b * b * g1 / den, b * b * g0 / den, b / den


def line_block(g_ref, faces_ref, start, size):
    alpha0, alpha1, _ = joint(g_ref, faces_ref)
    group = start // 128
    offset = start - group * 128
    rows = g_ref[group, pl.ds(pl.multiple_of(offset, size), size), :]
    low = group == 0
    edge_row = jnp.where(low, g_ref[0, 127:128, :], g_ref[1, 0:1, :])
    edge_col = jnp.where(low, rows[:, 127:128], rows[:, 0:1])
    alpha = jnp.where(low, alpha0, alpha1)
    block = rows + (alpha * edge_col) * edge_row
    return pltpu.roll(block, lax.rem(128 - offset, 128), 1)


def element(g_ref, joined, i, j):
    alpha0, alpha1, beta = joined
    gi, gj = i // 128, j // 128
    li, lj = i % 128, j % 128
    ei, ej = (0 if gi else 127), (0 if gj else 127)
    across = g_ref[gi, li : li + 1, ei : ei + 1] * g_ref[gj, ej : ej + 1, lj : lj + 1]
    if gi == gj:
        alpha = alpha1 if gi else alpha0
        return g_ref[gi, li : li + 1, lj : lj + 1] + alpha * across
    return beta * across


MIB = 1024 * 1024


def call(kernel, out_shape, flops, nbytes, name, room=20, **kw):
    return pl.pallas_call(
        kernel,
        out_shape=out_shape,
        name=name,
        compiler_params=pltpu.CompilerParams(vmem_limit_bytes=int(room * MIB)),
        cost_estimate=pl.CostEstimate(flops=flops, bytes_accessed=nbytes, transcendentals=0),
        **kw,
    )


def call_after(earlier, kernel, out_shape, flops, nbytes, name, *args, **kw):
    count, extra = len(args), len(earlier)

    def ordered(*refs):
        kernel(*refs[:count], *refs[count + extra :])

    specs = [pl.BlockSpec(memory_space=pltpu.VMEM)] * count + [pl.BlockSpec(memory_space=pltpu.HBM)] * extra
    return call(ordered, out_shape, flops, nbytes, name, in_specs=specs, **kw)(*args, *earlier)


def explicit_kernel(
    u_hbm, r_hbm, xf_hbm, gy_hbm, yf_hbm, a_hbm, ends_ref,
    buf_ref, u_ref, r_ref, a_ref, xf_ref, gy_ref, yf_ref, f_ref, u_sem, r_sem, a_sem, s_sem
):
    planes, cells, width = u_ref.shape
    small = [
        pltpu.make_async_copy(gy_hbm, gy_ref, s_sem.at[0]),
        pltpu.make_async_copy(yf_hbm, yf_ref, s_sem.at[1]),
        pltpu.make_async_copy(xf_hbm, xf_ref, s_sem.at[2]),
    ]
    for copy in small:
        copy.start()

    def fetch(z):
        return (
            pltpu.make_async_copy(u_hbm.at[z], u_ref.at[z], u_sem.at[z]),
            pltpu.make_async_copy(r_hbm.at[z], r_ref.at[z], r_sem.at[z]),
        )

    def give(z):
        return pltpu.make_async_copy(a_ref.at[z], a_hbm.at[z], a_sem.at[z])

    for z in range(planes):
        for copy in fetch(z):
            copy.start()
    for copy in small:
        copy.wait()

    block = line_block(gy_ref, yf_ref, lax.axis_index("row") * cells, cells)
    last = block[:, cells - 1 : cells] / block[cells - 1 : cells, cells - 1 : cells]
    first = block[:, 0:1] / block[0:1, 0:1]
    w = [jnp.broadcast_to(v, (cells, LANES)) for v in (last, first)]
    here = time_step * xf_ref[...]
    lane = iota((1, width), 1)
    after = jnp.where(lane == width - 1, 0.0, pltpu.roll(here, width - 1, 1))
    f_ref[0:1, :] = after
    f_ref[1:2, :] = jnp.where(lane == 0, 0.0, here)
    f_ref[2:3, :] = 4.0 - (after + here)

    span = buf_ref.shape[2]
    count = width // LANES
    lane = iota((cells, LANES), 1)

    def plane(z, carry):
        for copy in fetch(z):
            copy.wait()

        def column(c):
            here = u_ref[z, :, c * LANES : (c + 1) * LANES]
            return here, pltpu.roll(here, 1, 1), pltpu.roll(here, LANES - 1, 1)

        sums = {}
        before = jnp.zeros((cells, LANES), F32)
        now = column(0)
        for c in range(count):
            then = column(c + 1) if c + 1 < count else (None, None, before)
            u = now[0]
            lower = jnp.where(lane == 0, before, now[1])
            upper = jnp.where(lane == LANES - 1, then[2], now[2])
            at = slice(c * LANES, (c + 1) * LANES)
            rate = r_ref[z, :, at] * (time_step - time_step * (u * u)) + f_ref[2:3, at]
            a = f_ref[0:1, at] * upper + f_ref[1:2, at] * lower + rate * u
            a_ref[z, :, at] = a
            for k in range(2):
                for f, field in enumerate((a, u)):
                    row = jnp.sum(w[k] * field, axis=0, keepdims=True)
                    sums.setdefault((k, f), []).append(row)
            if (c + 1) * LANES % span == 0:
                for (k, f), pieces in sums.items():
                    row = jnp.concatenate(pieces, axis=1)
                    buf_ref[c * LANES // span, pl.ds(z + 16 * k + 8 * f, 1), :] = row
                sums = {}
            before, now = now[1], then
        give(z).start()
        return carry

    lax.fori_loop(0, planes, plane, 0)
    for d in range(width // span):
        ends_ref[:, d * span : (d + 1) * span] = buf_ref[d]
    for z in range(planes):
        give(z).wait()


def coef_kernel(count, g_ref, f_ref, out_ref):
    joined = joint(g_ref, f_ref)
    size = 256 // count
    m = functools.partial(element, g_ref, joined)
    out_ref[...] = jnp.zeros_like(out_ref)
    for c in range(count):
        b, e = c * size, c * size + size - 1
        if c > 0:
            ee = m(e, e - size) / m(e, e)
            be = m(b, b - 1)
            out_ref[c : c + 1, :] = jnp.broadcast_to(ee, (1, LANES))
            out_ref[count + c : count + c + 1, :] = jnp.broadcast_to(be, (1, LANES))
        if c < count - 1:
            bb = m(b, b + size) / m(b, b)
            eb = m(e, e + 1)
            out_ref[2 * count + c : 2 * count + c + 1, :] = jnp.broadcast_to(bb, (1, LANES))
            out_ref[3 * count + c : 3 * count + c + 1, :] = jnp.broadcast_to(eb, (1, LANES))


def line_rows(g_ref, faces_ref, start, size):
    alpha0, alpha1, beta = joint(g_ref, faces_ref)
    group = start // 128
    offset = start - group * 128
    rows = g_ref[group, pl.ds(pl.multiple_of(offset, size), size), :]
    low = group == 0
    edge = jnp.where(low, rows[:, 127:128], rows[:, 0:1])
    end0, end1 = g_ref[0, 127:128, :], g_ref[1, 0:1, :]
    left = jnp.where(low, rows + (alpha0 * edge) * end0, (beta * edge) * end0)
    right = jnp.where(low, (beta * edge) * end1, rows + (alpha1 * edge) * end1)
    return left, right


def pair_kernel(cells, rings, mine_ref, got_ref, gy_ref, yf_ref, *out_refs):
    *send_refs, near_ref, mark_ref = out_refs
    mark_ref[...] = jnp.zeros_like(mark_ref)
    r = lax.axis_index("row")
    pair = r // 2
    lower = r % 2 == 0
    block = line_block(gy_ref, yf_ref, pair * (2 * cells), 2 * cells)
    e0, b1, e1 = cells - 1, cells, 2 * cells - 1
    up = block[e1 : e1 + 1, e0 : e0 + 1] / block[e1 : e1 + 1, e1 : e1 + 1]
    down = block[0:1, b1 : b1 + 1] / block[0:1, 0:1]
    cross = block[b1 : b1 + 1, e0 : e0 + 1]
    half = mine_ref.shape[0] // 2
    span = 512
    for s in range(mine_ref.shape[1] // span):
        at = slice(s * span, (s + 1) * span)
        p, p_got = mine_ref[:half, at], got_ref[:half, at]
        q, q_got = mine_ref[half:, at], got_ref[half:, at]
        p0, p1 = jnp.where(lower, p, p_got), jnp.where(lower, p_got, p)
        q0, q1 = jnp.where(lower, q, q_got), jnp.where(lower, q_got, q)
        below = p1 + up * p0
        above = q0 + down * q1
        for k, send_ref in enumerate(send_refs):
            send_ref[:, at] = jnp.where(pair + k + 1 < rings, below, above)
        near_ref[:half, at] = jnp.where(lower, 0.0, cross * p0)
        near_ref[half:, at] = jnp.where(lower, cross * q1, 0.0)


def scan_kernel(in_ref, c_ref, out_ref):
    count, rows, span = in_ref.shape
    half = rows // 2

    def coef(k):
        return c_ref[k : k + 1, 0:1]

    zero = jnp.zeros((half, span), F32)
    out_ref[0, :half, :] = zero
    out_ref[count - 1, half:, :] = zero
    below = above = None
    for s in range(count - 1):
        own = in_ref[s, :half, :]
        below = own if s == 0 else own + coef(s) * below
        out_ref[s + 1, :half, :] = coef(count + s + 1) * below
        t = count - 1 - s
        own = in_ref[t, half:, :]
        above = own if s == 0 else own + coef(2 * count + t) * above
        out_ref[t - 1, half:, :] = coef(3 * count + t - 1) * above


def local_kernel(
    a_hbm, u_hbm, gy_ref, yf_ref, gz_ref, zf_ref, l_hbm, zp_ref,
    k_ref, a_ref, u_ref, l_ref, a_sem, u_sem, l_sem
):
    chunks, planes, cells, span = u_ref.shape

    def fetch(k):
        lanes = pl.ds(pl.multiple_of(k * span, span), span)
        return (
            pltpu.make_async_copy(a_hbm.at[:, lanes], a_ref.at[k], a_sem.at[k]),
            pltpu.make_async_copy(u_hbm.at[:, :, lanes], u_ref.at[k], u_sem.at[k]),
        )

    def give(k):
        lanes = pl.ds(pl.multiple_of(k * span, span), span)
        return pltpu.make_async_copy(l_ref.at[k], l_hbm.at[:, lanes], l_sem.at[k])

    for k in range(chunks):
        for copy in fetch(k):
            copy.start()
    count = k_ref.shape[0] // 2
    local = planes * cells

    dy = line_block(gy_ref, yf_ref, lax.axis_index("row") * cells, cells)
    dz = line_block(gz_ref, zf_ref, lax.axis_index(("chip", "core")) * planes, planes)
    spread_y = (iota((LANES, local), 0) == iota((LANES, local), 1) % cells).astype(F32)
    spread_z = (iota((LANES, local), 0) == iota((LANES, local), 1) // cells).astype(F32)
    dy_tiled = dot(dy, spread_y)
    unit = (iota((cells, local), 0) == iota((cells, local), 1) % cells).astype(F32)
    last = dz[planes - 1 : planes, :] / dz[planes - 1 : planes, planes - 1 : planes]
    first = dz[0:1, :] / dz[0:1, 0:1]
    rows = jnp.concatenate([dz, last, first, jnp.zeros((6, LANES), F32)], axis=0)
    wide = dot(rows, spread_z)
    plane = iota((1, local), 1) // cells

    def unit_part(k, row):
        other = unit * row
        return other + jnp.where(plane == k, dy_tiled, 0.0) if k < planes else other

    for k in range(planes + 2):
        row = wide[k : k + 1, :]
        own, rest = k * cells, count + k * cells
        for lanes, value in ((0, dy_tiled * row), (local, -2.0 * unit_part(k, row))):
            high, low = halves(value)
            k_ref[own : own + cells, lanes : lanes + local] = high
            k_ref[rest : rest + cells, lanes : lanes + local] = low

    def chunk(k, carry):
        for copy in fetch(k):
            copy.wait()
        both = jnp.concatenate(
            [a_ref[k], u_ref[k].reshape(local, span)], axis=0
        )
        high, low = halves(both)
        wide = jnp.dot(k_ref[...], high, preferred_element_type=F32)
        out = wide[:count] + wide[count:]
        out = out + jnp.dot(k_ref[:count], low, preferred_element_type=F32)
        l_ref[k] = out[:local, :]
        zp_ref[:, pl.ds(pl.multiple_of(k * span, span), span)] = out[local:, :]
        give(k).start()
        return carry

    lax.fori_loop(0, chunks, chunk, 0)
    for k in range(chunks):
        give(k).wait()


def reduced_kernel(g_ref, xf_ref, wh_ref, wl_ref, bh_ref, bl_ref, mark_ref):
    groups, width = g_ref.shape[0], g_ref.shape[1]
    order = 2 * groups
    shape = (order, LANES)
    row, col = iota(shape, 0), iota(shape, 1)
    current = ((row == col) | (row + order == col)).astype(F32)
    mark_ref[...] = jnp.zeros_like(mark_ref)
    couple = [half_step * xf_ref[0:1, width * c : width * c + 1] for c in range(1, groups)]
    lane = iota((width, LANES), 1)
    for c in range(groups):
        block = g_ref[c]
        ends = jnp.where(
            lane == 2 * c,
            block[:, 0:1],
            jnp.where(lane == 2 * c + 1, block[:, width - 1 : width], 0.0),
        )
        wh_ref[c, :, :width], wl_ref[c, :, :width] = halves(block)
        wh_ref[c, :, width:], wl_ref[c, :, width:] = halves(ends)
        first_row, last_row = g_ref[c, 0:1, :], g_ref[c, width - 1 : width, :]
        if c > 0:
            at = row == 2 * c - 1
            b = couple[c - 1]
            current = current - jnp.where(at & (col == 2 * c), b * first_row[:, 0:1], 0.0)
            current = current - jnp.where(at & (col == 2 * c + 1), b * last_row[:, 0:1], 0.0)
        if c < groups - 1:
            at = row == 2 * c + 2
            b = couple[c]
            current = current - jnp.where(
                at & (col == 2 * c), b * first_row[:, width - 1 : width], 0.0
            )
            current = current - jnp.where(
                at & (col == 2 * c + 1), b * last_row[:, width - 1 : width], 0.0
            )
    for s in range(order):
        pivot = current[s : s + 1, :] / current[s : s + 1, s : s + 1]
        current = jnp.where(row == s, pivot, current - current[:, s : s + 1] * pivot)
    for c in range(groups):
        span = slice(c * width, (c + 1) * width)
        add = jnp.zeros((order, width), F32)
        if c > 0:
            k = order + 2 * c - 1
            add = add + current[:, k : k + 1] * (couple[c - 1] * g_ref[c, 0:1, :])
        if c < groups - 1:
            k = order + 2 * c + 2
            add = add + current[:, k : k + 1] * (couple[c] * g_ref[c, width - 1 : width, :])
        bh_ref[:, span], bl_ref[:, span] = halves(add)


def dot_halves(both, high, left, right):
    count = high.shape[0]
    wide = jnp.dot(both, left, preferred_element_type=F32)
    return wide[:count] + wide[count:] + jnp.dot(high, right, preferred_element_type=F32)


def x_solve(rows_ref, wh_ref, wl_ref, bh_ref, bl_ref, out_ref, store):
    groups, width = wh_ref.shape[0], wh_ref.shape[1]
    ends = jnp.zeros((rows_ref.shape[0], LANES), F32)
    for c in range(groups):
        at = slice(c * width, (c + 1) * width)
        high, low = halves(rows_ref[:, at])
        wide = dot_halves(jnp.concatenate([high, low], axis=0), high, wh_ref[c], wl_ref[c])
        out_ref[:, at] = wide[:, :width]
        ends = ends + wide[:, width:]
    order = bh_ref.shape[0]
    high, low = halves(ends[:, :order])
    both = jnp.concatenate([high, low], axis=0)
    for c in range(groups // 2):
        at = slice(2 * c * width, 2 * (c + 1) * width)
        store(at, out_ref[:, at] + dot_halves(both, high, bh_ref[:, at], bl_ref[:, at]))


def section_kernel(
    near_ref, r1_ref, r2_ref, r3_ref, zp_ref, gy_ref, yf_ref, gz_ref, zf_ref,
    keep_ref, send_ref, rows_hbm, all_ref, rows_ref, sem
):
    rows, width = near_ref.shape
    cells = zp_ref.shape[0] // 2
    planes = rows // 4
    mine = lax.axis_index("core")
    r = lax.axis_index("row")
    pair = r // 2
    dy = line_block(gy_ref, yf_ref, r * cells, cells)
    dz = line_block(gz_ref, zf_ref, lax.axis_index(("chip", "core")) * planes, planes)
    from_last = dy[:, cells - 1 : cells] / dy[cells - 1 : cells, cells - 1 : cells]
    from_first = dy[:, 0:1] / dy[0:1, 0:1]
    last = dz[:, planes - 1 : planes] / dz[planes - 1 : planes, planes - 1 : planes]
    first = dz[:, 0:1] / dz[0:1, 0:1]
    full = line_rows(gy_ref, yf_ref, r * cells, cells)
    step = 2 * cells
    below, above = [], []
    for k in range(1, 4):
        lo = hi = jnp.zeros((1, 1), F32)
        for t in range(4):
            b, e = t * step % 128, t * step % 128 + step - 1
            part = full[t * step // 128]
            lo = jnp.where(pair - k == t, part[0:1, e : e + 1], lo)
            hi = jnp.where(pair - k + 4 == t, part[cells - 1 : cells, b : b + 1], hi)
        below.append(lo)
        above.append(hi)
    half = rows // 2
    span = 256
    for s in range(width // span):
        at = slice(s * span, (s + 1) * span)
        got = [ref[:, at] for ref in (r1_ref, r2_ref, r3_ref)]
        lo = near_ref[:half, at] + sum(c * g for c, g in zip(below, got))
        hi = near_ref[half:, at] + sum(c * g for c, g in zip(above, got))
        rows_ref[:half, at] = lo
        rows_ref[half:, at] = hi
    copy = pltpu.make_async_copy(rows_ref, rows_hbm, sem)
    copy.start()
    for s in range(width // span):
        at = slice(s * span, (s + 1) * span)
        lo, hi = rows_ref[:planes, at], rows_ref[half : half + planes, at]
        for k, w in enumerate((last, first)):
            low = jnp.sum(w * lo, axis=0, keepdims=True)
            high = jnp.sum(w * hi, axis=0, keepdims=True)
            own = slice(k * cells, (k + 1) * cells)
            all_ref[own, at] = zp_ref[own, at] + from_first * low + from_last * high
    half = cells // 2
    for k in range(2):
        at = slice(k * half, (k + 1) * half)
        kept = pl.multiple_of(k * cells + mine * half, half)
        sent = pl.multiple_of(k * cells + (1 - mine) * half, half)
        keep_ref[at, :] = all_ref[pl.ds(kept, half), :]
        send_ref[at, :] = all_ref[pl.ds(sent, half), :]
    copy.wait()


def chip_pair(keep_ref, recv_ref, rows, lanes):
    lower_core = lax.axis_index("core") == 0
    kept, got = keep_ref[rows, lanes], recv_ref[rows, lanes]
    return jnp.where(lower_core, kept, got), jnp.where(lower_core, got, kept)


def pack_kernel(planes, keep_ref, recv_ref, gz_ref, zf_ref, buf_ref, near_ref):
    chip = 2 * planes
    block = line_block(gz_ref, zf_ref, lax.axis_index("chip") * chip, chip)
    e0, e1 = planes - 1, chip - 1
    up = block[e1 : e1 + 1, e0 : e0 + 1] / block[e1 : e1 + 1, e1 : e1 + 1]
    down = block[0:1, planes : planes + 1] / block[0:1, 0:1]
    cross = block[planes : planes + 1, e0 : e0 + 1]
    dests, rows, span = buf_ref.shape
    half = rows // 2
    for d in range(dests):
        lanes = slice(d * span, (d + 1) * span)
        p0, p1 = chip_pair(keep_ref, recv_ref, slice(0, half), lanes)
        buf_ref[d, :half, :] = p1 + up * p0
        near_ref[:half, lanes] = cross * p0
        q0, q1 = chip_pair(keep_ref, recv_ref, slice(half, rows), lanes)
        buf_ref[d, half:, :] = q0 + down * q1
        near_ref[half:, lanes] = cross * q1


def unpack_kernel(planes, back_ref, near_ref, gz_ref, zf_ref, own_ref, sib_ref):
    chip = 2 * planes
    block = line_block(gz_ref, zf_ref, lax.axis_index("chip") * chip, chip)
    e0, b1, e1 = planes - 1, planes, chip - 1
    up = block[b1 : b1 + 1, 0:1] / block[0:1, 0:1]
    down = block[e0 : e0 + 1, e1 : e1 + 1] / block[e1 : e1 + 1, e1 : e1 + 1]
    lower_core = lax.axis_index("core") == 0
    dests, rows, span = back_ref.shape
    half = rows // 2
    for d in range(dests):
        lanes = slice(d * span, (d + 1) * span)
        below0 = back_ref[d, :half, :]
        below1 = up * below0 + near_ref[:half, lanes]
        above1 = back_ref[d, half:, :]
        above0 = down * above1 + near_ref[half:, lanes]
        own_ref[:half, lanes] = jnp.where(lower_core, below0, below1)
        own_ref[half:, lanes] = jnp.where(lower_core, above0, above1)
        sib_ref[:half, lanes] = jnp.where(lower_core, below1, below0)
        sib_ref[half:, lanes] = jnp.where(lower_core, above1, above0)


def inner_kernel(
    l_ref, y_ref, u_ref, gy_ref, yf_ref, gz_ref, zf_ref, wh_ref, wl_ref, bh_ref, bl_ref,
    out_ref, mark_ref, rows_ref, part_ref
):
    mark_ref[...] = jnp.zeros_like(mark_ref)
    rows, width = y_ref.shape
    planes = rows // 4
    cells = u_ref.shape[1]
    local = planes * cells
    dy = line_block(gy_ref, yf_ref, lax.axis_index("row") * cells, cells)
    dz = line_block(gz_ref, zf_ref, lax.axis_index(("chip", "core")) * planes, planes)
    from_last = dy[:, cells - 1 : cells] / dy[cells - 1 : cells, cells - 1 : cells]
    from_first = dy[:, 0:1] / dy[0:1, 0:1]
    lane = iota((1, LANES), 1)
    parts = []
    for z in range(planes):
        row = jnp.where(lane < planes, dz[z : z + 1, :], jnp.where(lane == planes + z, -2.0, 0.0))
        parts.append(from_first * row + from_last * pltpu.roll(row, 2 * planes, 1))
    high, low = halves(jnp.concatenate(parts, axis=0)[:, :rows])
    both = jnp.concatenate([high, low], axis=0)
    span = 256
    for s in range(width // span):
        at = slice(s * span, (s + 1) * span)
        y_high, y_low = halves(y_ref[:, at])
        wide = jnp.dot(both, y_high, preferred_element_type=F32)
        wide = wide[:local] + wide[local:] + jnp.dot(high, y_low, preferred_element_type=F32)
        rows_ref[:, at] = l_ref[:, at] + wide

    def store(at, value):
        for z in range(planes):
            out_ref[z, :, at] = u_ref[z, :, at] + value[z * cells : (z + 1) * cells, :]

    x_solve(rows_ref, wh_ref, wl_ref, bh_ref, bl_ref, part_ref, store)


def final_kernel(
    s_hbm, own_ref, got_ref, gz_ref, zf_ref, wh_ref, wl_ref, bh_ref, bl_ref,
    out_hbm, x_ref, sx_ref, f_ref, in_sem, out_sem
):
    planes, cells = f_ref.shape[0], f_ref.shape[1]
    half = cells // 2

    def fetch(z):
        return pltpu.make_async_copy(s_hbm.at[z], f_ref.at[z], in_sem.at[z])

    def give(z):
        return pltpu.make_async_copy(f_ref.at[z], out_hbm.at[z], out_sem.at[z])

    for z in range(planes):
        fetch(z).start()
    mine = lax.axis_index("core")
    for k in range(2):
        at = slice(k * half, (k + 1) * half)
        own = pl.multiple_of(k * cells + mine * half, half)
        other = pl.multiple_of(k * cells + (1 - mine) * half, half)
        x_ref[pl.ds(own, half), :] = own_ref[at, :]
        x_ref[pl.ds(other, half), :] = got_ref[at, :]
    dz = line_block(gz_ref, zf_ref, lax.axis_index(("chip", "core")) * planes, planes)
    first = dz[:, 0:1] / dz[0:1, 0:1]
    last = dz[:, planes - 1 : planes] / dz[planes - 1 : planes, planes - 1 : planes]

    def store(at, value):
        sx_ref[:, at] = value

    x_solve(x_ref, wh_ref, wl_ref, bh_ref, bl_ref, sx_ref, store)
    for z in range(planes):
        low, high = first[z : z + 1, :], last[z : z + 1, :]
        fetch(z).wait()
        f_ref[z] = f_ref[z] + low * sx_ref[:cells, :] + high * sx_ref[cells:, :]
        give(z).start()
    for z in range(planes):
        give(z).wait()


def body(scalar_field, reaction, x_faces, y_faces, z_faces, x_inverse, y_inverse, z_inverse):
    planes, cells, width = scalar_field.shape
    local = planes * cells
    rows = lax.axis_size("row")
    chips = lax.axis_size("chip")
    xf, yf, zf = x_faces[None, :], y_faces[None, :], z_faces[None, :]
    sds = lambda *s: jax.ShapeDtypeStruct(s, F32)
    held = lambda *s: pltpu.VMEM(s, F32)

    far = pl.BlockSpec(memory_space=pltpu.HBM)
    near_by = pl.BlockSpec(memory_space=pltpu.VMEM)
    field = pltpu.VMEM((planes, cells, width), F32)
    a, ends = call(
        explicit_kernel,
        (sds(planes, cells, width), held(4 * planes, width)),
        20 * local * width,
        12 * local * width,
        "explicit",
        in_specs=[far] * 5,
        out_specs=(far, near_by),
        scratch_shapes=[
            pltpu.VMEM((8, 4 * planes, width // 8), F32),
            field,
            field,
            field,
            pltpu.VMEM((1, width), F32),
            pltpu.VMEM((2, 128, 128), F32),
            pltpu.VMEM((1, 256), F32),
            pltpu.VMEM((8, width), F32),
            pltpu.SemaphoreType.DMA((planes,)),
            pltpu.SemaphoreType.DMA((planes,)),
            pltpu.SemaphoreType.DMA((planes,)),
            pltpu.SemaphoreType.DMA((3,)),
        ],
        room=60,
    )(scalar_field, reaction, xf, y_inverse, yf)
    got_ends = lax.ppermute(ends, "row", [(i, i ^ 1) for i in range(rows)])

    half = lambda *s: jax.ShapeDtypeStruct(s, BF16)
    *weights, x_made = call(
        reduced_kernel,
        (
            half(16, 128, 256),
            half(16, 128, 256),
            half(32, width),
            half(32, width),
            held(8, LANES),
        ),
        10**9,
        2 * 10**6,
        "reduced",
        room=60,
    )(x_inverse, xf)
    chunks = 4
    field_chunks = pltpu.VMEM((chunks, planes, cells, width // chunks), F32)
    inside, z_part = call(
        local_kernel,
        (sds(local, width), held(2 * cells, width)),
        6 * 320 * 512 * width,
        14 * local * width,
        "local",
        in_specs=[far, far] + [near_by] * 4,
        out_specs=(far, near_by),
        scratch_shapes=[
            pltpu.VMEM((2 * (local + 2 * cells), 2 * local), BF16),
            pltpu.VMEM((chunks, local, width // chunks), F32),
            field_chunks,
            pltpu.VMEM((chunks, local, width // chunks), F32),
            pltpu.SemaphoreType.DMA((chunks,)),
            pltpu.SemaphoreType.DMA((chunks,)),
            pltpu.SemaphoreType.DMA((chunks,)),
        ],
        input_output_aliases={0: 0},
        room=61.5,
    )(a.reshape(local, width), scalar_field, y_inverse, yf, z_inverse, zf)

    *sums, near_y, joined = call_after(
        (z_part,),
        functools.partial(pair_kernel, cells, rows // 2),
        tuple(sds(2 * planes, width) for _ in range(3))
        + (sds(4 * planes, width), held(8, LANES)),
        10**6,
        10**6,
        "pair",
        ends,
        got_ends,
        y_inverse,
        yf,
    )
    got_sums = [
        lax.ppermute(total, "row", [(i, (i + 2 * k + 2) % rows) for i in range(rows)])
        for k, total in enumerate(sums)
    ]

    z_coef = call_after(
        (joined,),
        functools.partial(coef_kernel, chips),
        held(4 * chips, LANES),
        10**8,
        10**6,
        "coefs",
        z_inverse,
        zf,
    )
    keep, send, y_rows = call_after(
        (z_coef,),
        section_kernel,
        (sds(cells, width), sds(cells, width), pltpu.HBM((4 * planes, width), F32)),
        10**7,
        10**6,
        "section",
        near_y,
        *got_sums,
        z_part,
        y_inverse,
        yf,
        z_inverse,
        zf,
        out_specs=(near_by, near_by, far),
        scratch_shapes=[
            pltpu.VMEM((2 * cells, width), F32),
            pltpu.VMEM((4 * planes, width), F32),
            pltpu.SemaphoreType.DMA,
        ],
    )
    pairs = [(0, 1), (1, 0)]
    recv = lax.ppermute(send, "core", pairs)
    z_buf, near = call(
        functools.partial(pack_kernel, planes),
        (sds(chips, cells, width // chips), sds(cells, width)),
        10**6,
        10**6,
        "pack",
    )(keep, recv, z_inverse, zf)
    z_in = lax.all_to_all(z_buf, "chip", 0, 0, tiled=True)

    z_out = call_after(
        (x_made,), scan_kernel, sds(*z_in.shape), 10**6, 10**6, "scan_z", z_in, z_coef
    )
    z_back = lax.all_to_all(z_out, "chip", 0, 0, tiled=True)
    partial_out, inner_made = call(
        inner_kernel,
        (sds(planes, cells, width), held(8, LANES)),
        12 * local * width * 200,
        16 * local * width,
        "inner",
        scratch_shapes=[pltpu.VMEM((local, width), F32), pltpu.VMEM((local, width), F32)],
        room=60,
    )(inside, y_rows, scalar_field, y_inverse, yf, z_inverse, zf, *weights)
    own, sib = call_after(
        (inner_made,),
        functools.partial(unpack_kernel, planes),
        (sds(cells, width), sds(cells, width)),
        10**6,
        10**6,
        "unpack",
        z_back,
        near,
        z_inverse,
        zf,
    )
    got = lax.ppermute(sib, "core", pairs)
    return call(
        final_kernel,
        sds(planes, cells, width),
        12 * local * width,
        8 * local * width,
        "final",
        in_specs=[far] + [near_by] * 8,
        out_specs=far,
        scratch_shapes=[
            pltpu.VMEM((2 * cells, width), F32),
            pltpu.VMEM((2 * cells, width), F32),
            field,
            pltpu.SemaphoreType.DMA((planes,)),
            pltpu.SemaphoreType.DMA((planes,)),
        ],
        input_output_aliases={0: 0},
    )(partial_out, own, got, z_inverse, zf, *weights)


def solution(mesh):
    rows, columns = mesh.shape["row"], mesh.shape["col"]
    split = Mesh(mesh.devices.reshape(rows, columns // 2, 2), ("row", "chip", "core"))
    field = P(("chip", "core"), "row", None)
    in_specs = (field, field, P(), P(), P(), P(), P(), P())
    return jax.shard_map(body, mesh=split, in_specs=in_specs, out_specs=field, check_vma=False)
```

```python
import functools

import jax
import jax.numpy as jnp
from jax import lax
from jax.experimental import pallas as pl
from jax.experimental.pallas import tpu as pltpu
from jax.sharding import Mesh
from jax.sharding import PartitionSpec as P

F32 = jnp.float32
BF16 = jnp.bfloat16
half_step = 500.0
time_step = 1000.0
LANES = 128


def dot(left, right):
    return lax.dot_general(
        left,
        right,
        (((1,), (0,)), ((), ())),
        precision=lax.Precision.HIGHEST,
        preferred_element_type=F32,
    )


def halves(value):
    high = value.astype(BF16)
    return high, (value - high.astype(F32)).astype(BF16)


def iota(shape, dim):
    return lax.broadcasted_iota(jnp.int32, shape, dim)


def joint(g_ref, faces_ref):
    b = half_step * faces_ref[0:1, 128:129]
    g0 = g_ref[0, 127:128, 127:128]
    g1 = g_ref[1, 0:1, 0:1]
    den = 1.0 - b * b * g0 * g1
    return b * b * g1 / den, b * b * g0 / den, b / den


def line_block(g_ref, faces_ref, start, size):
    alpha0, alpha1, _ = joint(g_ref, faces_ref)
    group = start // 128
    offset = start - group * 128
    rows = g_ref[group, pl.ds(pl.multiple_of(offset, size), size), :]
    low = group == 0
    edge_row = jnp.where(low, g_ref[0, 127:128, :], g_ref[1, 0:1, :])
    edge_col = jnp.where(low, rows[:, 127:128], rows[:, 0:1])
    alpha = jnp.where(low, alpha0, alpha1)
    block = rows + (alpha * edge_col) * edge_row
    return pltpu.roll(block, lax.rem(128 - offset, 128), 1)


def element(g_ref, joined, i, j):
    alpha0, alpha1, beta = joined
    gi, gj = i // 128, j // 128
    li, lj = i % 128, j % 128
    ei, ej = (0 if gi else 127), (0 if gj else 127)
    across = g_ref[gi, li : li + 1, ei : ei + 1] * g_ref[gj, ej : ej + 1, lj : lj + 1]
    if gi == gj:
        alpha = alpha1 if gi else alpha0
        return g_ref[gi, li : li + 1, lj : lj + 1] + alpha * across
    return beta * across


MIB = 1024 * 1024


def call(kernel, out_shape, flops, nbytes, name, room=20, **kw):
    return pl.pallas_call(
        kernel,
        out_shape=out_shape,
        name=name,
        compiler_params=pltpu.CompilerParams(vmem_limit_bytes=int(room * MIB)),
        cost_estimate=pl.CostEstimate(flops=flops, bytes_accessed=nbytes, transcendentals=0),
        **kw,
    )


def call_after(earlier, kernel, out_shape, flops, nbytes, name, *args, **kw):
    count, extra = len(args), len(earlier)

    def ordered(*refs):
        kernel(*refs[:count], *refs[count + extra :])

    specs = [pl.BlockSpec(memory_space=pltpu.VMEM)] * count + [pl.BlockSpec(memory_space=pltpu.HBM)] * extra
    return call(ordered, out_shape, flops, nbytes, name, in_specs=specs, **kw)(*args, *earlier)


def explicit_kernel(
    u_hbm, r_hbm, xf_hbm, gy_hbm, yf_hbm, a_hbm, ends_ref,
    buf_ref, u_ref, r_ref, a_ref, xf_ref, gy_ref, yf_ref, f_ref, u_sem, r_sem, a_sem, s_sem
):
    planes, cells, width = u_ref.shape
    small = [
        pltpu.make_async_copy(gy_hbm, gy_ref, s_sem.at[0]),
        pltpu.make_async_copy(yf_hbm, yf_ref, s_sem.at[1]),
        pltpu.make_async_copy(xf_hbm, xf_ref, s_sem.at[2]),
    ]
    def fetch(z):
        return (
            pltpu.make_async_copy(u_hbm.at[z], u_ref.at[z], u_sem.at[z]),
            pltpu.make_async_copy(r_hbm.at[z], r_ref.at[z], r_sem.at[z]),
        )

    def give(z):
        return pltpu.make_async_copy(a_ref.at[z], a_hbm.at[z], a_sem.at[z])

    for copy in small[:2] + list(fetch(0)) + small[2:]:
        copy.start()
    for z in range(1, planes):
        for copy in fetch(z):
            copy.start()
    for copy in small:
        copy.wait()

    block = line_block(gy_ref, yf_ref, lax.axis_index("row") * cells, cells)
    last = block[:, cells - 1 : cells] / block[cells - 1 : cells, cells - 1 : cells]
    first = block[:, 0:1] / block[0:1, 0:1]
    w = [jnp.broadcast_to(v, (cells, LANES)) for v in (last, first)]
    here = time_step * xf_ref[...]
    lane = iota((1, width), 1)
    after = jnp.where(lane == width - 1, 0.0, pltpu.roll(here, width - 1, 1))
    f_ref[0:1, :] = after
    f_ref[1:2, :] = jnp.where(lane == 0, 0.0, here)
    f_ref[2:3, :] = 4.0 - (after + here)

    span = buf_ref.shape[2]
    count = width // LANES
    lane = iota((cells, LANES), 1)

    def plane(z, carry):
        for copy in fetch(z):
            copy.wait()

        def column(c):
            here = u_ref[z, :, c * LANES : (c + 1) * LANES]
            return here, pltpu.roll(here, 1, 1), pltpu.roll(here, LANES - 1, 1)

        sums = {}
        before = jnp.zeros((cells, LANES), F32)
        now = column(0)
        for c in range(count):
            then = column(c + 1) if c + 1 < count else (None, None, before)
            u = now[0]
            lower = jnp.where(lane == 0, before, now[1])
            upper = jnp.where(lane == LANES - 1, then[2], now[2])
            at = slice(c * LANES, (c + 1) * LANES)
            rate = r_ref[z, :, at] * (time_step - time_step * (u * u)) + f_ref[2:3, at]
            a = f_ref[0:1, at] * upper + f_ref[1:2, at] * lower + rate * u
            a_ref[z, :, at] = a
            for k in range(2):
                for f, field in enumerate((a, u)):
                    row = jnp.sum(w[k] * field, axis=0, keepdims=True)
                    sums.setdefault((k, f), []).append(row)
            if (c + 1) * LANES % span == 0:
                for (k, f), pieces in sums.items():
                    row = jnp.concatenate(pieces, axis=1)
                    buf_ref[c * LANES // span, pl.ds(z + 16 * k + 8 * f, 1), :] = row
                sums = {}
            before, now = now[1], then
        give(z).start()
        return carry

    lax.fori_loop(0, planes, plane, 0)
    for d in range(width // span):
        ends_ref[:, d * span : (d + 1) * span] = buf_ref[d]
    for z in range(planes):
        give(z).wait()


def coef_kernel(count, g_ref, f_ref, out_ref):
    joined = joint(g_ref, f_ref)
    size = 256 // count
    m = functools.partial(element, g_ref, joined)
    out_ref[...] = jnp.zeros_like(out_ref)
    for c in range(count):
        b, e = c * size, c * size + size - 1
        if c > 0:
            ee = m(e, e - size) / m(e, e)
            be = m(b, b - 1)
            out_ref[c : c + 1, :] = jnp.broadcast_to(ee, (1, LANES))
            out_ref[count + c : count + c + 1, :] = jnp.broadcast_to(be, (1, LANES))
        if c < count - 1:
            bb = m(b, b + size) / m(b, b)
            eb = m(e, e + 1)
            out_ref[2 * count + c : 2 * count + c + 1, :] = jnp.broadcast_to(bb, (1, LANES))
            out_ref[3 * count + c : 3 * count + c + 1, :] = jnp.broadcast_to(eb, (1, LANES))


def line_rows(g_ref, faces_ref, start, size):
    alpha0, alpha1, beta = joint(g_ref, faces_ref)
    group = start // 128
    offset = start - group * 128
    rows = g_ref[group, pl.ds(pl.multiple_of(offset, size), size), :]
    low = group == 0
    edge = jnp.where(low, rows[:, 127:128], rows[:, 0:1])
    end0, end1 = g_ref[0, 127:128, :], g_ref[1, 0:1, :]
    left = jnp.where(low, rows + (alpha0 * edge) * end0, (beta * edge) * end0)
    right = jnp.where(low, (beta * edge) * end1, rows + (alpha1 * edge) * end1)
    return left, right


def pair_kernel(cells, rings, mine_ref, got_ref, gy_ref, yf_ref, *out_refs):
    *send_refs, near_ref, mark_ref = out_refs
    mark_ref[...] = jnp.zeros_like(mark_ref)
    r = lax.axis_index("row")
    pair = r // 2
    lower = r % 2 == 0
    block = line_block(gy_ref, yf_ref, pair * (2 * cells), 2 * cells)
    e0, b1, e1 = cells - 1, cells, 2 * cells - 1
    up = block[e1 : e1 + 1, e0 : e0 + 1] / block[e1 : e1 + 1, e1 : e1 + 1]
    down = block[0:1, b1 : b1 + 1] / block[0:1, 0:1]
    cross = block[b1 : b1 + 1, e0 : e0 + 1]
    half = mine_ref.shape[0] // 2
    span = 512
    for s in range(mine_ref.shape[1] // span):
        at = slice(s * span, (s + 1) * span)
        p, p_got = mine_ref[:half, at], got_ref[:half, at]
        q, q_got = mine_ref[half:, at], got_ref[half:, at]
        p0, p1 = jnp.where(lower, p, p_got), jnp.where(lower, p_got, p)
        q0, q1 = jnp.where(lower, q, q_got), jnp.where(lower, q_got, q)
        below = p1 + up * p0
        above = q0 + down * q1
        for k, send_ref in enumerate(send_refs):
            send_ref[:, at] = jnp.where(pair + k + 1 < rings, below, above)
        near_ref[:half, at] = jnp.where(lower, 0.0, cross * p0)
        near_ref[half:, at] = jnp.where(lower, cross * q1, 0.0)


def scan_kernel(in_ref, c_ref, out_ref):
    count, rows, span = in_ref.shape
    half = rows // 2

    def coef(k):
        return c_ref[k : k + 1, 0:1]

    zero = jnp.zeros((half, span), F32)
    out_ref[0, :half, :] = zero
    out_ref[count - 1, half:, :] = zero
    below = above = None
    for s in range(count - 1):
        own = in_ref[s, :half, :]
        below = own if s == 0 else own + coef(s) * below
        out_ref[s + 1, :half, :] = coef(count + s + 1) * below
        t = count - 1 - s
        own = in_ref[t, half:, :]
        above = own if s == 0 else own + coef(2 * count + t) * above
        out_ref[t - 1, half:, :] = coef(3 * count + t - 1) * above


def local_kernel(
    a_hbm, u_hbm, gy_ref, yf_ref, gz_ref, zf_ref, l_hbm, zp_ref,
    k_ref, a_ref, u_ref, l_ref, a_sem, u_sem, l_sem
):
    chunks, planes, cells, span = u_ref.shape

    def fetch(k):
        lanes = pl.ds(pl.multiple_of(k * span, span), span)
        return (
            pltpu.make_async_copy(a_hbm.at[:, lanes], a_ref.at[k], a_sem.at[k]),
            pltpu.make_async_copy(u_hbm.at[:, :, lanes], u_ref.at[k], u_sem.at[k]),
        )

    def give(k):
        lanes = pl.ds(pl.multiple_of(k * span, span), span)
        return pltpu.make_async_copy(l_ref.at[k], l_hbm.at[:, lanes], l_sem.at[k])

    for k in range(chunks):
        for copy in fetch(k):
            copy.start()
    count = k_ref.shape[0] // 2
    local = planes * cells

    dy = line_block(gy_ref, yf_ref, lax.axis_index("row") * cells, cells)
    dz = line_block(gz_ref, zf_ref, lax.axis_index(("chip", "core")) * planes, planes)
    spread_y = (iota((LANES, local), 0) == iota((LANES, local), 1) % cells).astype(F32)
    spread_z = (iota((LANES, local), 0) == iota((LANES, local), 1) // cells).astype(F32)
    dy_tiled = dot(dy, spread_y)
    unit = (iota((cells, local), 0) == iota((cells, local), 1) % cells).astype(F32)
    last = dz[planes - 1 : planes, :] / dz[planes - 1 : planes, planes - 1 : planes]
    first = dz[0:1, :] / dz[0:1, 0:1]
    rows = jnp.concatenate([dz, last, first, jnp.zeros((6, LANES), F32)], axis=0)
    wide = dot(rows, spread_z)
    plane = iota((1, local), 1) // cells

    def unit_part(k, row):
        other = unit * row
        return other + jnp.where(plane == k, dy_tiled, 0.0) if k < planes else other

    for k in range(planes + 2):
        row = wide[k : k + 1, :]
        own, rest = k * cells, count + k * cells
        for lanes, value in ((0, dy_tiled * row), (local, -2.0 * unit_part(k, row))):
            high, low = halves(value)
            k_ref[own : own + cells, lanes : lanes + local] = high
            k_ref[rest : rest + cells, lanes : lanes + local] = low

    def chunk(k, carry):
        for copy in fetch(k):
            copy.wait()
        both = jnp.concatenate(
            [a_ref[k], u_ref[k].reshape(local, span)], axis=0
        )
        high, low = halves(both)
        wide = jnp.dot(k_ref[...], high, preferred_element_type=F32)
        out = wide[:count] + wide[count:]
        out = out + jnp.dot(k_ref[:count], low, preferred_element_type=F32)
        l_ref[k] = out[:local, :]
        zp_ref[:, pl.ds(pl.multiple_of(k * span, span), span)] = out[local:, :]
        give(k).start()
        return carry

    lax.fori_loop(0, chunks, chunk, 0)
    for k in range(chunks):
        give(k).wait()


def reduced_kernel(g_ref, xf_ref, wh_ref, wl_ref, bh_ref, bl_ref, mark_ref):
    groups, width = g_ref.shape[0], g_ref.shape[1]
    order = 2 * groups
    shape = (order, LANES)
    row, col = iota(shape, 0), iota(shape, 1)
    current = ((row == col) | (row + order == col)).astype(F32)
    mark_ref[...] = jnp.zeros_like(mark_ref)
    couple = [half_step * xf_ref[0:1, width * c : width * c + 1] for c in range(1, groups)]
    lane = iota((width, LANES), 1)
    for c in range(groups):
        block = g_ref[c]
        ends = jnp.where(
            lane == 2 * c,
            block[:, 0:1],
            jnp.where(lane == 2 * c + 1, block[:, width - 1 : width], 0.0),
        )
        wh_ref[c, :, :width], wl_ref[c, :, :width] = halves(block)
        wh_ref[c, :, width:], wl_ref[c, :, width:] = halves(ends)
        first_row, last_row = g_ref[c, 0:1, :], g_ref[c, width - 1 : width, :]
        if c > 0:
            at = row == 2 * c - 1
            b = couple[c - 1]
            current = current - jnp.where(at & (col == 2 * c), b * first_row[:, 0:1], 0.0)
            current = current - jnp.where(at & (col == 2 * c + 1), b * last_row[:, 0:1], 0.0)
        if c < groups - 1:
            at = row == 2 * c + 2
            b = couple[c]
            current = current - jnp.where(
                at & (col == 2 * c), b * first_row[:, width - 1 : width], 0.0
            )
            current = current - jnp.where(
                at & (col == 2 * c + 1), b * last_row[:, width - 1 : width], 0.0
            )
    for s in range(order):
        pivot = current[s : s + 1, :] / current[s : s + 1, s : s + 1]
        current = jnp.where(row == s, pivot, current - current[:, s : s + 1] * pivot)
    for c in range(groups):
        span = slice(c * width, (c + 1) * width)
        add = jnp.zeros((order, width), F32)
        if c > 0:
            k = order + 2 * c - 1
            add = add + current[:, k : k + 1] * (couple[c - 1] * g_ref[c, 0:1, :])
        if c < groups - 1:
            k = order + 2 * c + 2
            add = add + current[:, k : k + 1] * (couple[c] * g_ref[c, width - 1 : width, :])
        bh_ref[:, span], bl_ref[:, span] = halves(add)


def dot_halves(both, high, left, right):
    count = high.shape[0]
    wide = jnp.dot(both, left, preferred_element_type=F32)
    return wide[:count] + wide[count:] + jnp.dot(high, right, preferred_element_type=F32)


def x_solve(rows_ref, wh_ref, wl_ref, bh_ref, bl_ref, out_ref, store):
    groups, width = wh_ref.shape[0], wh_ref.shape[1]
    ends = jnp.zeros((rows_ref.shape[0], LANES), F32)
    for c in range(groups):
        at = slice(c * width, (c + 1) * width)
        high, low = halves(rows_ref[:, at])
        wide = dot_halves(jnp.concatenate([high, low], axis=0), high, wh_ref[c], wl_ref[c])
        out_ref[:, at] = wide[:, :width]
        ends = ends + wide[:, width:]
    order = bh_ref.shape[0]
    high, low = halves(ends[:, :order])
    both = jnp.concatenate([high, low], axis=0)
    for c in range(groups // 2):
        at = slice(2 * c * width, 2 * (c + 1) * width)
        store(at, out_ref[:, at] + dot_halves(both, high, bh_ref[:, at], bl_ref[:, at]))


def section_kernel(
    near_ref, r1_ref, r2_ref, r3_ref, zp_ref, gy_ref, yf_ref, gz_ref, zf_ref,
    keep_ref, send_ref, rows_hbm, all_ref, rows_ref, sem
):
    rows, width = near_ref.shape
    cells = zp_ref.shape[0] // 2
    planes = rows // 4
    mine = lax.axis_index("core")
    r = lax.axis_index("row")
    pair = r // 2
    dy = line_block(gy_ref, yf_ref, r * cells, cells)
    dz = line_block(gz_ref, zf_ref, lax.axis_index(("chip", "core")) * planes, planes)
    from_last = dy[:, cells - 1 : cells] / dy[cells - 1 : cells, cells - 1 : cells]
    from_first = dy[:, 0:1] / dy[0:1, 0:1]
    last = dz[:, planes - 1 : planes] / dz[planes - 1 : planes, planes - 1 : planes]
    first = dz[:, 0:1] / dz[0:1, 0:1]
    full = line_rows(gy_ref, yf_ref, r * cells, cells)
    step = 2 * cells
    below, above = [], []
    for k in range(1, 4):
        lo = hi = jnp.zeros((1, 1), F32)
        for t in range(4):
            b, e = t * step % 128, t * step % 128 + step - 1
            part = full[t * step // 128]
            lo = jnp.where(pair - k == t, part[0:1, e : e + 1], lo)
            hi = jnp.where(pair - k + 4 == t, part[cells - 1 : cells, b : b + 1], hi)
        below.append(lo)
        above.append(hi)
    half = rows // 2
    span = 256
    for s in range(width // span):
        at = slice(s * span, (s + 1) * span)
        got = [ref[:, at] for ref in (r1_ref, r2_ref, r3_ref)]
        lo = near_ref[:half, at] + sum(c * g for c, g in zip(below, got))
        hi = near_ref[half:, at] + sum(c * g for c, g in zip(above, got))
        rows_ref[:half, at] = lo
        rows_ref[half:, at] = hi
    copy = pltpu.make_async_copy(rows_ref, rows_hbm, sem)
    copy.start()
    for s in range(width // span):
        at = slice(s * span, (s + 1) * span)
        lo, hi = rows_ref[:planes, at], rows_ref[half : half + planes, at]
        for k, w in enumerate((last, first)):
            low = jnp.sum(w * lo, axis=0, keepdims=True)
            high = jnp.sum(w * hi, axis=0, keepdims=True)
            own = slice(k * cells, (k + 1) * cells)
            all_ref[own, at] = zp_ref[own, at] + from_first * low + from_last * high
    half = cells // 2
    for k in range(2):
        at = slice(k * half, (k + 1) * half)
        kept = pl.multiple_of(k * cells + mine * half, half)
        sent = pl.multiple_of(k * cells + (1 - mine) * half, half)
        keep_ref[at, :] = all_ref[pl.ds(kept, half), :]
        send_ref[at, :] = all_ref[pl.ds(sent, half), :]
    copy.wait()


def chip_pair(keep_ref, recv_ref, rows, lanes):
    lower_core = lax.axis_index("core") == 0
    kept, got = keep_ref[rows, lanes], recv_ref[rows, lanes]
    return jnp.where(lower_core, kept, got), jnp.where(lower_core, got, kept)


def pack_kernel(planes, keep_ref, recv_ref, gz_ref, zf_ref, buf_ref, near_ref):
    chip = 2 * planes
    block = line_block(gz_ref, zf_ref, lax.axis_index("chip") * chip, chip)
    e0, e1 = planes - 1, chip - 1
    up = block[e1 : e1 + 1, e0 : e0 + 1] / block[e1 : e1 + 1, e1 : e1 + 1]
    down = block[0:1, planes : planes + 1] / block[0:1, 0:1]
    cross = block[planes : planes + 1, e0 : e0 + 1]
    dests, rows, span = buf_ref.shape
    half = rows // 2
    for d in range(dests):
        lanes = slice(d * span, (d + 1) * span)
        p0, p1 = chip_pair(keep_ref, recv_ref, slice(0, half), lanes)
        buf_ref[d, :half, :] = p1 + up * p0
        near_ref[:half, lanes] = cross * p0
        q0, q1 = chip_pair(keep_ref, recv_ref, slice(half, rows), lanes)
        buf_ref[d, half:, :] = q0 + down * q1
        near_ref[half:, lanes] = cross * q1


def unpack_kernel(planes, back_ref, near_ref, gz_ref, zf_ref, own_ref, sib_ref):
    chip = 2 * planes
    block = line_block(gz_ref, zf_ref, lax.axis_index("chip") * chip, chip)
    e0, b1, e1 = planes - 1, planes, chip - 1
    up = block[b1 : b1 + 1, 0:1] / block[0:1, 0:1]
    down = block[e0 : e0 + 1, e1 : e1 + 1] / block[e1 : e1 + 1, e1 : e1 + 1]
    lower_core = lax.axis_index("core") == 0
    dests, rows, span = back_ref.shape
    half = rows // 2
    for d in range(dests):
        lanes = slice(d * span, (d + 1) * span)
        below0 = back_ref[d, :half, :]
        below1 = up * below0 + near_ref[:half, lanes]
        above1 = back_ref[d, half:, :]
        above0 = down * above1 + near_ref[half:, lanes]
        own_ref[:half, lanes] = jnp.where(lower_core, below0, below1)
        own_ref[half:, lanes] = jnp.where(lower_core, above0, above1)
        sib_ref[:half, lanes] = jnp.where(lower_core, below1, below0)
        sib_ref[half:, lanes] = jnp.where(lower_core, above1, above0)


def inner_kernel(
    l_ref, y_ref, u_ref, gy_ref, yf_ref, gz_ref, zf_ref, wh_ref, wl_ref, bh_ref, bl_ref,
    out_ref, mark_ref, rows_ref, part_ref
):
    mark_ref[...] = jnp.zeros_like(mark_ref)
    rows, width = y_ref.shape
    planes = rows // 4
    cells = u_ref.shape[1]
    local = planes * cells
    dy = line_block(gy_ref, yf_ref, lax.axis_index("row") * cells, cells)
    dz = line_block(gz_ref, zf_ref, lax.axis_index(("chip", "core")) * planes, planes)
    from_last = dy[:, cells - 1 : cells] / dy[cells - 1 : cells, cells - 1 : cells]
    from_first = dy[:, 0:1] / dy[0:1, 0:1]
    lane = iota((1, LANES), 1)
    parts = []
    for z in range(planes):
        row = jnp.where(lane < planes, dz[z : z + 1, :], jnp.where(lane == planes + z, -2.0, 0.0))
        parts.append(from_first * row + from_last * pltpu.roll(row, 2 * planes, 1))
    high, low = halves(jnp.concatenate(parts, axis=0)[:, :rows])
    both = jnp.concatenate([high, low], axis=0)
    span = 256
    for s in range(width // span):
        at = slice(s * span, (s + 1) * span)
        y_high, y_low = halves(y_ref[:, at])
        wide = jnp.dot(both, y_high, preferred_element_type=F32)
        wide = wide[:local] + wide[local:] + jnp.dot(high, y_low, preferred_element_type=F32)
        rows_ref[:, at] = l_ref[:, at] + wide

    def store(at, value):
        for z in range(planes):
            out_ref[z, :, at] = u_ref[z, :, at] + value[z * cells : (z + 1) * cells, :]

    x_solve(rows_ref, wh_ref, wl_ref, bh_ref, bl_ref, part_ref, store)


def final_kernel(
    s_hbm, own_ref, got_ref, gz_ref, zf_ref, wh_ref, wl_ref, bh_ref, bl_ref,
    out_hbm, x_ref, sx_ref, f_ref, in_sem, out_sem
):
    planes, cells = f_ref.shape[0], f_ref.shape[1]
    half = cells // 2

    def fetch(z):
        return pltpu.make_async_copy(s_hbm.at[z], f_ref.at[z], in_sem.at[z])

    def give(z):
        return pltpu.make_async_copy(f_ref.at[z], out_hbm.at[z], out_sem.at[z])

    for z in range(planes):
        fetch(z).start()
    mine = lax.axis_index("core")
    for k in range(2):
        at = slice(k * half, (k + 1) * half)
        own = pl.multiple_of(k * cells + mine * half, half)
        other = pl.multiple_of(k * cells + (1 - mine) * half, half)
        x_ref[pl.ds(own, half), :] = own_ref[at, :]
        x_ref[pl.ds(other, half), :] = got_ref[at, :]
    dz = line_block(gz_ref, zf_ref, lax.axis_index(("chip", "core")) * planes, planes)
    first = dz[:, 0:1] / dz[0:1, 0:1]
    last = dz[:, planes - 1 : planes] / dz[planes - 1 : planes, planes - 1 : planes]

    def store(at, value):
        sx_ref[:, at] = value

    x_solve(x_ref, wh_ref, wl_ref, bh_ref, bl_ref, sx_ref, store)
    for z in range(planes):
        low, high = first[z : z + 1, :], last[z : z + 1, :]
        fetch(z).wait()
        f_ref[z] = f_ref[z] + low * sx_ref[:cells, :] + high * sx_ref[cells:, :]
        give(z).start()
    for z in range(planes):
        give(z).wait()


def body(scalar_field, reaction, x_faces, y_faces, z_faces, x_inverse, y_inverse, z_inverse):
    planes, cells, width = scalar_field.shape
    local = planes * cells
    rows = lax.axis_size("row")
    chips = lax.axis_size("chip")
    xf, yf, zf = x_faces[None, :], y_faces[None, :], z_faces[None, :]
    sds = lambda *s: jax.ShapeDtypeStruct(s, F32)
    held = lambda *s: pltpu.VMEM(s, F32)

    far = pl.BlockSpec(memory_space=pltpu.HBM)
    near_by = pl.BlockSpec(memory_space=pltpu.VMEM)
    field = pltpu.VMEM((planes, cells, width), F32)
    a, ends = call(
        explicit_kernel,
        (sds(planes, cells, width), held(4 * planes, width)),
        20 * local * width,
        12 * local * width,
        "explicit",
        in_specs=[far] * 5,
        out_specs=(far, near_by),
        scratch_shapes=[
            pltpu.VMEM((8, 4 * planes, width // 8), F32),
            field,
            field,
            field,
            pltpu.VMEM((1, width), F32),
            pltpu.VMEM((2, 128, 128), F32),
            pltpu.VMEM((1, 256), F32),
            pltpu.VMEM((8, width), F32),
            pltpu.SemaphoreType.DMA((planes,)),
            pltpu.SemaphoreType.DMA((planes,)),
            pltpu.SemaphoreType.DMA((planes,)),
            pltpu.SemaphoreType.DMA((3,)),
        ],
        room=60,
    )(scalar_field, reaction, xf, y_inverse, yf)
    got_ends = lax.ppermute(ends, "row", [(i, i ^ 1) for i in range(rows)])

    half = lambda *s: jax.ShapeDtypeStruct(s, BF16)
    *weights, x_made = call(
        reduced_kernel,
        (
            half(16, 128, 256),
            half(16, 128, 256),
            half(32, width),
            half(32, width),
            held(8, LANES),
        ),
        10**9,
        2 * 10**6,
        "reduced",
        room=60,
    )(x_inverse, xf)
    chunks = 4
    field_chunks = pltpu.VMEM((chunks, planes, cells, width // chunks), F32)
    inside, z_part = call(
        local_kernel,
        (sds(local, width), held(2 * cells, width)),
        6 * 320 * 512 * width,
        14 * local * width,
        "local",
        in_specs=[far, far] + [near_by] * 4,
        out_specs=(far, near_by),
        scratch_shapes=[
            pltpu.VMEM((2 * (local + 2 * cells), 2 * local), BF16),
            pltpu.VMEM((chunks, local, width // chunks), F32),
            field_chunks,
            pltpu.VMEM((chunks, local, width // chunks), F32),
            pltpu.SemaphoreType.DMA((chunks,)),
            pltpu.SemaphoreType.DMA((chunks,)),
            pltpu.SemaphoreType.DMA((chunks,)),
        ],
        input_output_aliases={0: 0},
        room=61.5,
    )(a.reshape(local, width), scalar_field, y_inverse, yf, z_inverse, zf)

    *sums, near_y, joined = call_after(
        (z_part,),
        functools.partial(pair_kernel, cells, rows // 2),
        tuple(sds(2 * planes, width) for _ in range(3))
        + (sds(4 * planes, width), held(8, LANES)),
        10**6,
        10**6,
        "pair",
        ends,
        got_ends,
        y_inverse,
        yf,
    )
    got_sums = [
        lax.ppermute(total, "row", [(i, (i + 2 * k + 2) % rows) for i in range(rows)])
        for k, total in enumerate(sums)
    ]

    z_coef = call_after(
        (joined,),
        functools.partial(coef_kernel, chips),
        held(4 * chips, LANES),
        10**8,
        10**6,
        "coefs",
        z_inverse,
        zf,
    )
    keep, send, y_rows = call_after(
        (z_coef,),
        section_kernel,
        (sds(cells, width), sds(cells, width), pltpu.HBM((4 * planes, width), F32)),
        10**7,
        10**6,
        "section",
        near_y,
        *got_sums,
        z_part,
        y_inverse,
        yf,
        z_inverse,
        zf,
        out_specs=(near_by, near_by, far),
        scratch_shapes=[
            pltpu.VMEM((2 * cells, width), F32),
            pltpu.VMEM((4 * planes, width), F32),
            pltpu.SemaphoreType.DMA,
        ],
    )
    pairs = [(0, 1), (1, 0)]
    recv = lax.ppermute(send, "core", pairs)
    z_buf, near = call(
        functools.partial(pack_kernel, planes),
        (held(chips, cells, width // chips), sds(cells, width)),
        10**6,
        10**6,
        "pack",
    )(keep, recv, z_inverse, zf)
    z_in = lax.all_to_all(z_buf, "chip", 0, 0, tiled=True)

    z_out = call_after(
        (x_made,), scan_kernel, sds(*z_in.shape), 10**6, 10**6, "scan_z", z_in, z_coef
    )
    z_back = lax.all_to_all(z_out, "chip", 0, 0, tiled=True)
    partial_out, inner_made = call(
        inner_kernel,
        (sds(planes, cells, width), held(8, LANES)),
        12 * local * width * 200,
        16 * local * width,
        "inner",
        scratch_shapes=[pltpu.VMEM((local, width), F32), pltpu.VMEM((local, width), F32)],
        room=60,
    )(inside, y_rows, scalar_field, y_inverse, yf, z_inverse, zf, *weights)
    own, sib = call_after(
        (inner_made,),
        functools.partial(unpack_kernel, planes),
        (sds(cells, width), sds(cells, width)),
        10**6,
        10**6,
        "unpack",
        z_back,
        near,
        z_inverse,
        zf,
    )
    got = lax.ppermute(sib, "core", pairs)
    return call(
        final_kernel,
        sds(planes, cells, width),
        12 * local * width,
        8 * local * width,
        "final",
        in_specs=[far] + [near_by] * 8,
        out_specs=far,
        scratch_shapes=[
            pltpu.VMEM((2 * cells, width), F32),
            pltpu.VMEM((2 * cells, width), F32),
            field,
            pltpu.SemaphoreType.DMA((planes,)),
            pltpu.SemaphoreType.DMA((planes,)),
        ],
        input_output_aliases={0: 0},
    )(partial_out, own, got, z_inverse, zf, *weights)


def solution(mesh):
    rows, columns = mesh.shape["row"], mesh.shape["col"]
    split = Mesh(mesh.devices.reshape(rows, columns // 2, 2), ("row", "chip", "core"))
    field = P(("chip", "core"), "row", None)
    in_specs = (field, field, P(), P(), P(), P(), P(), P())
    return jax.shard_map(body, mesh=split, in_specs=in_specs, out_specs=field, check_vma=False)
```
